256 devices in a mesh: shard: 32 (over x_lo, z, core), rep: 8 (over y, x_hi).
Axes of the slice: x: 4 (x_hi: 2, x_lo: 2; x = x_hi * 2 + x_lo), y: 4, z: 8, core: 2. Of those that a mesh axis runs over, the one named last changes fastest.
Arguments:
- tokens: bfloat16 [2, 256, 128, 768], P(None, ('shard', 'rep')), may hold values from -6 to 6
- cotangent: bfloat16 [2, 256, 128, 768], P(None, ('shard', 'rep')), may hold values from -6 to 6
- picture_lengths: int32 [2, 256, 4], P(None, ('shard', 'rep')), may hold values from 1 to 64, 128 in all within a row
- w_qkv: float32 [2, 768, 2304], P(None, 'shard'), may hold values from -0.21875 to 0.21875
- mom_qkv: float32 [2, 768, 2304], P(None, 'shard'), may hold values from -6 to 6
- ema_qkv: float32 [2, 768, 2304], P(None, 'shard'), may hold values from -0.0009765625 to 0.0009765625
- w_out: float32 [2, 768, 768], P(None, 'shard'), may hold values from -0.875 to 0.875
- mom_out: float32 [2, 768, 768], P(None, 'shard'), may hold values from -4 to 4
- ema_out: float32 [2, 768, 768], P(None, 'shard'), may hold values from -0.00390625 to 0.00390625
- w_up: float32 [2, 768, 3072], P(None, 'shard'), may hold values from -0.21875 to 0.21875
- mom_up: float32 [2, 768, 3072], P(None, 'shard'), may hold values from -4 to 4
- ema_up: float32 [2, 768, 3072], P(None, 'shard'), may hold values from -0.0009765625 to 0.0009765625
- w_down: float32 [2, 3072, 768], P(None, 'shard'), may hold values from -0.109375 to 0.109375
- mom_down: float32 [2, 3072, 768], P(None, 'shard'), may hold values from -6 to 6
- ema_down: float32 [2, 3072, 768], P(None, 'shard'), may hold values from -0.00048828125 to 0.00048828125
- norms: float32 [2, 3200], P(None, 'shard'), may hold values from -0.5 to 1.6
- mom_norms: float32 [2, 3200], P(None, 'shard'), may hold values from -6 to 6
- ema_norms: float32 [2, 3200], P(None, 'shard'), may hold values from -0.0025 to 0.008
Outputs:
- activations: bfloat16 [2, 256, 128, 768], P(None, ('shard', 'rep'))
- input_grad: bfloat16 [2, 256, 128, 768], P(None, ('shard', 'rep'))
- new_qkv: float32 [2, 768, 2304], P(None, 'shard')
- new_mom_qkv: float32 [2, 768, 2304], P(None, 'shard')
- new_ema_qkv: float32 [2, 768, 2304], P(None, 'shard')
- copy_qkv: bfloat16 [2, 768, 2304], P(None, 'shard')
- new_out: float32 [2, 768, 768], P(None, 'shard')
- new_mom_out: float32 [2, 768, 768], P(None, 'shard')
- new_ema_out: float32 [2, 768, 768], P(None, 'shard')
- copy_out: bfloat16 [2, 768, 768], P(None, 'shard')
- new_up: float32 [2, 768, 3072], P(None, 'shard')
- new_mom_up: float32 [2, 768, 3072], P(None, 'shard')
- new_ema_up: float32 [2, 768, 3072], P(None, 'shard')
- copy_up: bfloat16 [2, 768, 3072], P(None, 'shard')
- new_down: float32 [2, 3072, 768], P(None, 'shard')
- new_mom_down: float32 [2, 3072, 768], P(None, 'shard')
- new_ema_down: float32 [2, 3072, 768], P(None, 'shard')
- copy_down: bfloat16 [2, 3072, 768], P(None, 'shard')
- new_norms: float32 [2, 3200], P(None, 'shard')
- new_mom_norms: float32 [2, 3200], P(None, 'shard')
- new_ema_norms: float32 [2, 3200], P(None, 'shard')
- copy_norms: bfloat16 [2, 3200], P(None, 'shard')
- shift_gradient: float32 [2, 768], P(None, 'shard')
The draws below stay inside these ranges and needn't reach their ends.
Inputs may be any that keep to these rules, and one draw needn't show every extreme that they name: `picture_lengths`: each row's lengths sum to 128.
All inputs are finite; a program needn't handle non-finite values.
Results may differ from the reference program's by a relative error of at most 0.03.
Values may be sent and summed in bfloat16 or wider, within the bound.
A program may use at most 256 MiB of HBM per device.

```python
import math
import jax
import jax.numpy as jnp
import numpy as np
from jax import lax

D = 768
HEADS = 12
HD = 64
FF = 3072
LAYERS = 2
MICRO = 2
ROW = 128
PICS = 4
SEQS = 256
TOKENS = 65536
NORM_WIDTH = 3200


def norm_table(key):
    keys_all = jax.random.split(key, 6)
    gain_one = jax.random.uniform(keys_all[0], (LAYERS, D), jnp.float32, 0.7, 1.3)
    bias_one = jax.random.uniform(keys_all[1], (LAYERS, D), jnp.float32, -0.5, 0.5)
    gain_two = jax.random.uniform(keys_all[2], (LAYERS, D), jnp.float32, 0.7, 1.3)
    bias_two = jax.random.uniform(keys_all[3], (LAYERS, D), jnp.float32, -0.5, 0.5)
    gain_query = jax.random.uniform(keys_all[4], (LAYERS, HD), jnp.float32, 1.0, 1.6)
    gain_key = jax.random.uniform(keys_all[5], (LAYERS, HD), jnp.float32, 1.0, 1.6)
    return jnp.concatenate([gain_one, bias_one, gain_two, bias_two, gain_query, gain_key], 1)


def draw_norms(key, part):
    key = jax.random.fold_in(key, 11)
    return norm_table(key)


def draw_ema_norms(key, part):
    key = jax.random.fold_in(key, 23)
    return 0.005 * norm_table(key)


def levels(own_key, extent, cuts, least, top_value):
    loudness, own = 1.0, jax.random.fold_in(own_key, 6)
    for axis_at, shards_of in cuts:
        draws = jnp.exp(jax.random.uniform(jax.random.fold_in(own, axis_at), (shards_of,), jnp.float32, least / len(cuts), top_value / len(cuts)))
        loudness = loudness * jnp.repeat(draws, extent[axis_at] // shards_of).reshape([-1 if axis == axis_at else 1 for axis in range(len(extent))])
    return loudness


def length_profile(amount, total, bound, lean):
    portions = [(1 << 20) // math.isqrt(rank ** lean) + 1 for rank in range(2, amount + 1)]
    rest, given = total - bound - (amount - 1), [1] * (amount - 1)
    while rest > 0:
        free = [i for i in range(amount - 1) if given[i] < bound]
        pool, left = sum([portions[i] for i in free]), rest
        for i in free:
            addition = min(bound - given[i], max(1, left * portions[i] // pool), rest)
            given[i] = given[i] + addition
            rest = rest - addition
    return np.array([bound] + given)


def ragged(rng, number_of, total, limit, skew):
    if number_of == 2:
        one = jax.random.randint(rng, (), max(1, total - limit), min(limit, total - 1) + 1)
        return jnp.stack([one, total - one])
    tallies = jnp.asarray(length_profile(number_of, total, limit, skew), jnp.int32)
    twos = (number_of - 1) // 2
    donor, taker = tallies[1:1 + 2 * twos:2], tallies[2:2 + 2 * twos:2]
    margin = jnp.minimum(donor - 1, limit - taker)
    shifted = jax.random.randint(jax.random.fold_in(rng, 1), (twos,), 0, 1 << 20) % (margin + 1)
    tallies = tallies.at[1:1 + 2 * twos:2].set(donor - shifted).at[2:2 + 2 * twos:2].set(taker + shifted)
    return tallies[jax.random.permutation(jax.random.fold_in(rng, 2), number_of)]


def normal_values(key, shape, scale, limit, cuts=(), kind=jnp.bfloat16):
    values = jax.random.normal(key, shape, jnp.float32) * scale
    if len(cuts) > 0:
        values = levels(key, shape, cuts, -0.22, 0.18) * values
    return jnp.clip(values, min=-limit, max=limit).astype(kind)


def setup_inputs(seed: int = 0) -> dict:
    arg_keys = jax.random.split(jax.random.key(seed), 19)
    tokens = normal_values(arg_keys[0], (MICRO, SEQS, ROW, D), 1.0, 6.0, ((1, 256),))
    cotangent = normal_values(arg_keys[1], (MICRO, SEQS, ROW, D), 1.0, 6.0, ((1, 256),))
    picture_lengths = jax.vmap(lambda own: ragged(own, PICS, ROW, ROW // 2, 2))(jax.random.split(arg_keys[2], MICRO * SEQS)).reshape((MICRO, SEQS, PICS)).astype(jnp.int32)
    w_qkv = normal_values(arg_keys[3], (LAYERS, D, 3 * D), D ** -0.5, 0.21875, ((1, 32),), jnp.float32)
    mom_qkv = normal_values(arg_keys[4], (LAYERS, D, 3 * D), 0.5, 6.0, ((1, 32),), jnp.float32)
    ema_qkv = normal_values(arg_keys[5], (LAYERS, D, 3 * D), (40000 * D) ** -0.5, 0.0009765625, ((1, 32),), jnp.float32)
    w_out = normal_values(arg_keys[6], (LAYERS, D, D), (D // 16) ** -0.5, 0.875, ((1, 32),), jnp.float32)
    mom_out = normal_values(arg_keys[7], (LAYERS, D, D), 0.3, 4.0, ((1, 32),), jnp.float32)
    ema_out = normal_values(arg_keys[8], (LAYERS, D, D), (40000 * (D // 16)) ** -0.5, 0.00390625, ((1, 32),), jnp.float32)
    w_up = normal_values(arg_keys[9], (LAYERS, D, FF), D ** -0.5, 0.21875, ((1, 32),), jnp.float32)
    mom_up = normal_values(arg_keys[10], (LAYERS, D, FF), 0.3, 4.0, ((1, 32),), jnp.float32)
    ema_up = normal_values(arg_keys[11], (LAYERS, D, FF), (40000 * D) ** -0.5, 0.0009765625, ((1, 32),), jnp.float32)
    w_down = normal_values(arg_keys[12], (LAYERS, FF, D), FF ** -0.5, 0.109375, ((1, 32),), jnp.float32)
    mom_down = normal_values(arg_keys[13], (LAYERS, FF, D), 0.6, 6.0, ((1, 32),), jnp.float32)
    ema_down = normal_values(arg_keys[14], (LAYERS, FF, D), (40000 * FF) ** -0.5, 0.00048828125, ((1, 32),), jnp.float32)
    norms = draw_norms(jax.random.fold_in(arg_keys[18], 71), 0)
    mom_norms = normal_values(arg_keys[16], (LAYERS, NORM_WIDTH), 1.0, 6.0, ((1, 32),), jnp.float32)
    ema_norms = draw_ema_norms(jax.random.fold_in(arg_keys[18], 71), 0)
    return {"tokens": tokens, "cotangent": cotangent, "picture_lengths": picture_lengths, "w_qkv": w_qkv, "mom_qkv": mom_qkv, "ema_qkv": ema_qkv, "w_out": w_out, "mom_out": mom_out, "ema_out": ema_out, "w_up": w_up, "mom_up": mom_up, "ema_up": ema_up, "w_down": w_down, "mom_down": mom_down, "ema_down": ema_down, "norms": norms, "mom_norms": mom_norms, "ema_norms": ema_norms}


highest = lax.Precision.HIGHEST
eps = 1e-06
momentum_decay = 0.9
average_decay = 0.99
learn_rate = 0.03

@jax.custom_vjp
def low(v):
    return lax.optimization_barrier(v.astype(jnp.bfloat16)).astype(jnp.float32)

@jax.custom_vjp
def low_back(v):
    return v

def low_keep(v):
    return (low(v), None)

def low_pass(kept, grad):
    return (grad,)

def back_keep(v):
    return (v, None)

def back_low(kept, grad):
    return (low(grad),)
low.defvjp(low_keep, low_pass)
low_back.defvjp(back_keep, back_low)

def layer_norm(values, scale_gain, shift_bias):
    center = values - lax.optimization_barrier(jnp.mean(values, -1, keepdims=True))
    spread = lax.optimization_barrier(jnp.mean(center * center, -1, keepdims=True))
    return center * lax.rsqrt(spread + eps) * scale_gain + shift_bias

def head_norm(values, scale_gain):
    center = values - lax.optimization_barrier(jnp.mean(values, -1, keepdims=True))
    spread = lax.optimization_barrier(jnp.mean(center * center, -1, keepdims=True))
    return center * lax.rsqrt(spread + eps) * scale_gain

def segment_ids(lengths):
    picture_ends = jnp.cumsum(lengths, -1)
    places = jnp.arange(ROW, dtype=jnp.int32)
    return lax.optimization_barrier(jnp.sum((places[None, :, None] >= picture_ends[:, None, :]).astype(jnp.int32), -1))

def layer_block(stream, same_picture, weights):
    w_qkv, w_out, w_up, w_down, norm_params = weights
    row_count = stream.shape[0]
    normed = low(layer_norm(stream, norm_params[0:D], norm_params[D:2 * D]))
    joined = low_back(jnp.einsum('rtd,de->rte', normed, w_qkv, precision=highest))
    joined = joined.reshape(row_count, ROW, 3, HEADS, HD)
    queries = low(head_norm(joined[:, :, 0], norm_params[4 * D:4 * D + HD]))
    keys_low = low(head_norm(joined[:, :, 1], norm_params[4 * D + HD:]))
    values_low = low(joined[:, :, 2])
    scores = jnp.einsum('rqhd,rkhd->rhqk', queries, keys_low, precision=highest) * HD ** (-0.5)
    scores = low_back(jnp.where(same_picture, scores, -1e+30))
    row_top = lax.optimization_barrier(jnp.max(scores, -1, keepdims=True))
    exponent = jnp.exp(scores - row_top)
    probability = low(exponent / lax.optimization_barrier(jnp.sum(exponent, -1, keepdims=True)))
    mixed = jnp.einsum('rhqk,rkhd->rqhd', probability, values_low, precision=highest)
    mixed = low(low_back(mixed.reshape(row_count, ROW, D)))
    middle = stream + low_back(jnp.einsum('rtd,de->rte', mixed, w_out, precision=highest))
    second = low(layer_norm(middle, norm_params[2 * D:3 * D], norm_params[3 * D:4 * D]))
    before = low_back(jnp.einsum('rtd,df->rtf', second, w_up, precision=highest))
    hidden = low(jax.nn.gelu(before))
    return middle + low_back(jnp.einsum('rtf,fd->rtd', hidden, w_down, precision=highest))

def forward(weights, stream, same_picture):
    lowered = [low(master) for master in weights]
    for layer_index in range(LAYERS):
        stream = layer_block(stream, same_picture, tuple((item[layer_index] for item in lowered)))
    return stream

def add_up(left_sum, right_sum):
    return left_sum + right_sum

def reference(tokens, cotangent, picture_lengths, w_qkv, mom_qkv, ema_qkv, w_out, mom_out, ema_out, w_up, mom_up, ema_up, w_down, mom_down, ema_down, norms, mom_norms, ema_norms):
    masters = (w_qkv, w_out, w_up, w_down, norms)
    total_rows = MICRO * SEQS
    group_rows = math.gcd(total_rows, max(1, 4096 // ROW))
    group_count = total_rows // group_rows

    def regroup(array):
        return array.reshape((group_count, group_rows) + array.shape[2:])

    def accumulate(totals, group_in):
        stream_in, cot_in, length_in = group_in
        segments = segment_ids(length_in)
        same_picture = (segments[:, :, None] == segments[:, None, :])[:, None]

        def run(weights, stream):
            return forward(weights, stream, same_picture)
        result, pull = jax.vjp(run, masters, stream_in.astype(jnp.float32))
        grads, back_grad = pull(cot_in.astype(jnp.float32))
        totals = jax.tree.map(add_up, totals, grads)
        return (totals, (result.astype(jnp.bfloat16), back_grad.astype(jnp.bfloat16)))
    start = tuple((jnp.zeros(master.shape, jnp.float32) for master in masters))
    totals, (results, back_grads) = lax.scan(accumulate, start, (regroup(tokens), regroup(cotangent), regroup(picture_lengths)))
    factor = TOKENS ** (-0.5)
    outputs = [results.reshape(MICRO, SEQS, ROW, D), back_grads.reshape(MICRO, SEQS, ROW, D)]
    moments = (mom_qkv, mom_out, mom_up, mom_down, mom_norms)
    averages = (ema_qkv, ema_out, ema_up, ema_down, ema_norms)
    for master, moment, average, gradient_sum in zip(masters, moments, averages, totals):
        gradient_scaled = gradient_sum * factor
        moment_new = momentum_decay * moment + gradient_scaled
        master_new = master - learn_rate * (gradient_scaled + momentum_decay * moment_new)
        average_new = average_decay * average + (1.0 - average_decay) * master_new
        outputs.extend([master_new, moment_new, average_new, master_new.astype(jnp.bfloat16)])
    outputs.append(totals[4][:, 3 * D:4 * D] * factor)
    return tuple(outputs)
```

```python
import math
from types import SimpleNamespace

import jax
import jax.numpy as jnp
from jax import lax
from jax.experimental import pallas as pl
from jax.experimental.pallas import tpu as pltpu
from jax.sharding import PartitionSpec as P

D = 768
HEADS = 12
HD = 64
FF = 3072
LAYERS = 2
ROWS = 256
PAIRS = HEADS // 2
CHUNK = 64
FOURTH = 768
RING = 8
BLOCK = 48
DBLOCK = 192
WIDE = 6144
HALF = 1536
QUARTER = 128
C_START, C_WIDTH = 512, 384
A_START, A_WIDTH = 1280, 256
STARTS = {"qkvo": 0, "up": 4 * D}
KINDS = ("qkvo", "up", "down")
PLACES = {off: off + 3 for off in range(-3, 5)} | {-4: 7}
GROUPS = ((3, None), (2, 4), (1, 5), (0, 6), (None, 7))
MESH = pl.DeviceIdType.MESH
BF = jnp.bfloat16
F32 = jnp.float32
NT = (((1,), (1,)), ((), ()))
NN = (((1,), (0,)), ((), ()))
TN = (((0,), (0,)), ((), ()))

eps = 1e-06
momentum_decay = 0.9
average_decay = 0.99
learn_rate = 0.03


class Place:
    def __init__(self):
        shard, rep = lax.axis_index("shard"), lax.axis_index("rep")
        self.c = shard % 2
        self.z = (shard // 2) % 8
        self.xl = shard // 16
        self.xh = rep % 2
        self.y = rep // 2
        self.x = self.xh * 2 + self.xl
        self.ys = [(self.y + d) % 4 for d in range(4)]
        self.xs = [((self.x + d) % 2, (self.x + d) % 4 // 2) for d in range(4)]

    def on_y(self, d):
        return self.ys[d % 4]

    def on_x(self, d):
        return self.xs[d % 4]

    def at(self, x=None, y=None, z=None, c=None):
        x = self.x if x is None else x
        y = self.y if y is None else y
        z = self.z if z is None else z
        c = self.c if c is None else c
        return (((x % 2) * 8 + z) * 2 + c, y * 2 + x // 2)

    def neighbours(self):
        sibling = self.at(c=1 - self.c)
        xs = {d: self.at(x=(self.x + d) % 4) for d in (1, -1, 2)}
        ys = {d: self.at(y=(self.y + d) % 4) for d in (1, -1, 2)}
        zs = {d: self.at(z=(self.z + d) % 8) for d in (1, -1)}
        return sibling, xs, ys, zs


class Net:
    def __init__(self, send, recv, someone, ruler):
        self.send, self.recv, self.someone, self.ruler = send, recv, someone, ruler
        self.count, self.sent = 0, []

    def copy(self, src, dst, device, at):
        return pltpu.make_async_remote_copy(
            src_ref=src,
            dst_ref=dst,
            send_sem=self.send.at[at],
            recv_sem=self.recv.at[at],
            device_id=device,
            device_id_type=MESH,
        )

    def reserve(self):
        self.count += 1
        assert self.count <= self.send.shape[0]
        return self.count - 1

    def put(self, src, dst, device):
        copy = self.copy(src, dst, device, self.reserve())
        copy.start()
        self.sent.append(copy)
        return copy

    def batch(self):
        self.sent.append(Batch(self))
        return self.sent[-1]

    def settle(self, most):
        for copy in self.sent[:most]:
            copy.wait_send()
        del self.sent[:most]

    def finish(self):
        self.settle(len(self.sent))


class Batch:
    def __init__(self, net):
        self.net, self.at, self.size = net, net.reserve(), 0

    def put(self, src, dst, device):
        self.net.copy(src, dst, device, self.at).start()
        self.size += math.prod(src.shape)

    def whole(self):
        tiles, ruler = self.size // 2048, self.net.ruler
        for blocks, depth in ((1, 16), (1, 48), (2, 48), (4, 48), (8, 48)):
            width, rest = divmod(tiles, blocks * (depth // 16))
            if rest == 0 and 128 * width <= ruler.shape[2]:
                view = ruler.at[0:blocks, 0:depth, 0 : 128 * width]
                return self.net.copy(view, view, self.net.someone, self.at)
        raise ValueError(tiles)

    def wait_recv(self):
        self.whole().wait_recv()

    def wait_send(self):
        self.whole().wait_send()


def place_of(zb, z):
    return (zb - z + PLACES[0] + 8) % 8


def greet(devices):
    barrier = pltpu.get_barrier_semaphore()
    for device in devices:
        pl.semaphore_signal(barrier, inc=1, device_id=device, device_id_type=MESH)
    return lambda: pl.semaphore_wait(barrier, len(devices))


def lanes(start, size):
    return pl.ds(pl.multiple_of(start, 128), size)


def rows16(start, size):
    return pl.ds(pl.multiple_of(start, 16), size)


def arrive(copies):
    for copy in copies:
        copy.wait_recv()


def dot(a, b, dims=NN):
    return lax.dot_general(a, b, dims, preferred_element_type=F32)


def by_rows(step, carry=0):
    def one(i, carry):
        return step(pl.ds(pl.multiple_of(i * CHUNK, CHUNK), CHUNK), carry)

    return lax.fori_loop(0, ROWS // CHUNK, one, carry)


def stats(values):
    center = values - jnp.mean(values, -1, keepdims=True)
    return center, lax.rsqrt(jnp.mean(center * center, -1, keepdims=True) + eps)


def fold(values):
    return jnp.sum(values.reshape(-1, 8, values.shape[-1]), 0)


def norm_into(out, source, gain, bias):
    def step(r, carry):
        center, scale = stats(source[r, :].astype(F32))
        out[r, :] = (center * scale * gain + bias).astype(BF)
        return carry

    by_rows(step)


def norm_back(source, slope, gain, grad, low):
    def step(r, carry):
        center, scale = stats(source[r, :].astype(F32))
        unit = center * scale
        up = slope[r, :]
        inner = up * gain
        inner_mean = jnp.mean(inner, -1, keepdims=True)
        along = jnp.mean(inner * unit, -1, keepdims=True)
        new = grad[r, :] + scale * (inner - inner_mean - unit * along)
        grad[r, :] = new
        low[r, :] = new.astype(BF)
        return carry[0] + fold(up * unit), carry[1] + fold(up)

    zero = jnp.zeros((8, D), F32)
    sums = by_rows(step, (zero, zero))
    return tuple(jnp.sum(s, 0, keepdims=True) for s in sums)


def head_mean(values, spread):
    high = values.astype(BF)
    low = (values - high.astype(F32)).astype(BF)
    return dot(jnp.concatenate([high, low], 1), spread)


def split_heads(values, first):
    zero = jnp.zeros_like(values)
    return jnp.concatenate([jnp.where(first, values, zero), jnp.where(first, zero, values)], 0)


def join_heads(values, first):
    half = values.shape[0] // 2
    return jnp.where(first, values[:half], values[half:])


def first_half(rows):
    return lax.broadcasted_iota(jnp.int32, (rows, 128), 1) < HD


def spread_matrix():
    a = lax.broadcasted_iota(jnp.int32, (256, 128), 0) // HD % 2
    b = lax.broadcasted_iota(jnp.int32, (256, 128), 1) // HD
    return jnp.where(a == b, 1.0 / HD, 0.0).astype(BF)


def make_masks(lengths, mask):
    at_row = lax.broadcasted_iota(jnp.int32, (128, 128), 0)
    at_col = lax.broadcasted_iota(jnp.int32, (128, 128), 1)
    for r in range(2):
        end = jnp.int32(0)
        left = jnp.zeros((128, 128), jnp.int32)
        right = jnp.zeros((128, 128), jnp.int32)
        for p in range(4):
            end = end + lengths[r, p]
            left = left + jnp.where(at_row >= end, 1, 0)
            right = right + jnp.where(at_col >= end, 1, 0)
        same = jnp.where(left == right, 1.0, 0.0)
        mask[r, 0:128, :] = same
        mask[r, 128:256, :] = same


def gelu_and_slope(before):
    inner_scale, cubic = 0.7978845608028654, 0.044715
    square = before * before
    tanh = jnp.tanh(inner_scale * before * (1.0 + cubic * square))
    half = 0.5 * (1.0 + tanh)
    slope = half + 0.5 * before * (1.0 - tanh * tanh) * inner_scale * (1.0 + 3.0 * cubic * square)
    return before * half, slope


def gain_rows(gains, layer):
    return tuple(gains[layer, i : i + 1, :] for i in range(6))


class Gather:
    def __init__(self, me, net, w1, wd, nz):
        self.me, self.net, self.w1, self.wd, self.nz = me, net, w1, wd, nz
        self.sibling, self.xs, self.ys, self.zs = me.neighbours()
        self.chunks = [self.chunk(layer, kind) for layer in range(LAYERS) for kind in KINDS]
        every = [(i, k) for i in range(len(self.chunks)) for k in range(7)]
        self.turns = sorted(every, key=lambda turn: (STARTS_AT[turn[0]] + turn[1], turn[0]))
        self.done = 0

    def chunk(self, layer, kind):
        me, w1, wd = self.me, self.w1, self.wd
        down = kind == "down"
        base = 96 * me.c if down else STARTS[kind] + HALF * me.c

        def q(at, k):
            if down:
                return wd.at[layer, :, at, rows16(base + 16 * k, 16), :]
            return w1.at[layer, :, at, :, lanes(base + QUARTER * k, QUARTER)]

        def p(at, k):
            if down:
                return wd.at[layer, k[0], at, rows16(base + 64 + 16 * k[1], 16), :]
            return w1.at[layer, k[0], at, :, lanes(base + C_START + C_WIDTH * k[1], C_WIDTH)]

        def a(at):
            return w1.at[layer, :, at, :, lanes(base + A_START, A_WIDTH)]

        def whole(at):
            if down:
                return wd.at[layer, :, at, rows16(base, 96), :]
            return w1.at[layer, :, at, :, lanes(base, HALF)]

        long = 1 if kind == "up" else -1
        pieces = [(lambda at: q(at, me.y), long), (lambda at: p(at, me.on_x(0)), -long)]
        return SimpleNamespace(
            pieces=pieces, fours=((q, me.on_y, self.ys), (p, me.on_x, self.xs)), whole=whole,
            spare=[] if down else [(a, 1)], norms=layer == 0 and kind == "qkvo", first={}, second=[],
            moving=None, aside=None, norm_moving=[], shared=None,
        )

    def ring(self, pieces, k):
        batch = self.net.batch()
        for view, long in pieces:
            for d in (1, -1):
                if k < 4 or d == long:
                    batch.put(view(PLACES[-d * (k - 1)]), view(PLACES[-d * k]), self.zs[d])
        return batch

    def norm_ring(self, k):
        copies = []
        for d in (1, -1):
            if k < 4 or d == 1:
                block = self.nz.at[(self.me.z - d * (k - 1) + 8) % 8]
                copies.append(self.net.put(block, block, self.zs[d]))
        return copies

    def spread(self, chunk, group):
        batch = self.net.batch()
        for at in GROUPS[group]:
            for view, place, devices in chunk.fours if at is not None else ():
                for d in (1, -1):
                    batch.put(view(at, place(0)), view(at, place(0)), devices[d])
        chunk.first[group] = batch

    def relay(self, chunk, group):
        chunk.first[group].wait_recv()
        batch = self.net.batch()
        for d, at in zip((1, -1), GROUPS[group]):
            for view, place, devices in chunk.fours if at is not None else ():
                block = view(at, place(-d))
                batch.put(block, block, devices[d])
        chunk.second.append(batch)

    def tick(self, chunk, k):
        if 1 <= k <= 4:
            chunk.moving.wait_recv()
            arrive(chunk.norm_moving)
        if k < 4:
            chunk.moving = self.ring(chunk.pieces, k + 1)
            chunk.norm_moving = self.norm_ring(k + 1) if chunk.norms else []
        if k < 5:
            self.spread(chunk, k)
        if 1 <= k <= 5:
            self.relay(chunk, k - 1)
        if chunk.spare and k >= 2:
            if k > 2:
                chunk.aside.wait_recv()
            if k <= 5:
                chunk.aside = self.ring(chunk.spare, k - 1)
        if k == 2:
            chunk.shared = self.net.batch()
        if k >= 2:
            chunk.second[k - 2].wait_recv()
            for at in GROUPS[k - 2]:
                if at is not None:
                    chunk.shared.put(chunk.whole(at), chunk.whole(at), self.sibling)

    def nudge(self):
        if self.done < len(self.turns):
            i, k = self.turns[self.done]
            self.tick(self.chunks[i], k)
            self.done += 1

    def complete(self, i):
        while (i, 6) not in self.turns[: self.done]:
            self.nudge()
        self.nudge()
        if i == len(self.chunks) - 1:
            self.net.settle(len(self.net.sent) - 4)
        self.chunks[i].shared.wait_recv()


STARTS_AT = (0, 0.5, 2.5, 3, 4, 4.5)
GATHER_COPIES = 130
SAVED = ("normed", "unit", "scales", "values", "probs", "mixed", "middle", "second", "hidden", "slope")


def forward_kernel(
    qkv_ref, out_ref, up_ref, wd_ref, norm_ref, tokens, lengths,
    act, w1_out, wd_out, gains, stream_out, *rest,
):
    saved_out, rest = dict(zip(SAVED, rest)), rest[len(SAVED) :]
    kept, rest = dict(zip(SAVED, rest)), rest[len(SAVED) :]
    w1, wd, xf, stream, mask, raw, line, nc, nx, nz, send, recv, local, out_sem, save_sem = rest
    normed, unit, scales, values, probs, mixed, middle, second, hidden, slope = (kept[name] for name in SAVED)
    me = Place()
    x, y, z, c, xl, xh = me.x, me.y, me.z, me.c, me.xl, me.xh
    sibling, xs, ys, zs = me.neighbours()
    met = greet([sibling, xs[1], xs[-1], ys[1], ys[-1], zs[1], zs[-1]])
    net = Net(send, recv, sibling, w1.at[0, 0])

    for i, kind in enumerate(STARTS):
        mine = xf.at[i, :, pl.ds(24 * c, 24), :]
        if kind == "up":
            pltpu.make_async_copy(up_ref.at[:, :, lanes(c * HALF, HALF)], mine, local.at[i]).start()
    nc[c] = jnp.zeros((56, 128), F32)
    line[...] = jnp.zeros((8, 256), F32)
    line[0:2, 0:100] = norm_ref[...].astype(BF).astype(F32)
    first = 100 * lax.axis_index("shard")
    for layer in range(LAYERS):
        row = pltpu.roll(jnp.broadcast_to(line[layer : layer + 1, :], (8, 256)), first % 128, 1)
        for i in range(2):
            nc[c, pl.ds(25 * layer + first // 128 + i, 1), :] = row[0:1, 128 * i : 128 * i + 128]
    own_q, own_h = rows16(16 * y, 16), rows16(64 + 16 * xh, 16)
    own_qd = wd.at[:, xl, PLACES[0], rows16(96 * c + 16 * y, 16), :]
    own_qd[...] = wd_ref[:, own_q, :].astype(BF)
    wd[:, xl, PLACES[0], rows16(96 * c + 64 + 16 * xh, 16), :] = wd_ref[:, own_h, :].astype(BF)
    make_masks(lengths, mask)
    met()
    norm_swap = net.put(nc.at[c], nc.at[c], sibling)
    arrivals = []
    for i, kind in enumerate(STARTS):
        mine = xf.at[i, :, pl.ds(24 * c, 24), :]
        if kind == "up":
            net.put(up_ref.at[:, :, lanes((1 - c) * HALF, HALF)], mine, sibling)
        else:
            at = net.reserve()

            def parts(core):
                if core == 0:
                    return [(qkv_ref.at[:, :, 0:HALF], mine)]
                return [
                    (qkv_ref.at[:, :, HALF : 3 * D], mine.at[:, :, 0:D]),
                    (out_ref, mine.at[:, :, D:HALF]),
                ]

            for core in range(2):

                @pl.when(c == core)
                def _():
                    for src, dst in parts(core):
                        pltpu.make_async_copy(src, dst, local.at[i]).start()
                    for src, dst in parts(1 - core):
                        net.copy(src, dst, sibling, at).start()

            net.sent.append(net.copy(mine, mine, sibling, at))
        arrivals.append((pltpu.make_async_copy(mine, mine, local.at[i]), net.sent[-1]))
    cross = [net.put(own_qd, own_qd, xs[-1])]
    norm_swap.wait_recv()
    nx[xl] = nc[0] + nc[1]
    cross.append(net.put(nx.at[xl], nx.at[xl], xs[1]))
    for i, start in enumerate(STARTS.values()):
        base = start + c * HALF
        arrivals[i][0].wait()
        arrivals[i][1].wait_recv()
        own_q1 = w1.at[:, xl, PLACES[0], :, lanes(base + QUARTER * y, QUARTER)]
        own_a1 = w1.at[:, xl, PLACES[0], :, lanes(base + A_START, A_WIDTH)]
        own_q1[...] = xf[i, :, :, lanes(QUARTER * y, QUARTER)].astype(BF)
        own_a1[...] = xf[i, :, :, A_START : A_START + A_WIDTH].astype(BF)
        cross.append(net.put(own_q1, own_q1, xs[1]))
        cross.append(net.put(own_a1, own_a1, xs[-1]))
        w1[:, xl, PLACES[0], :, lanes(base + C_START + C_WIDTH * xh, C_WIDTH)] = xf[
            i, :, :, lanes(C_START + C_WIDTH * xh, C_WIDTH)
        ].astype(BF)
    arrive(cross)
    nz[z] = nx[0] + nx[1]
    moves = Gather(me, net, w1, wd, nz)
    outs = []

    def out(src, dst, sem):
        outs.append(pltpu.make_async_copy(src, dst, sem))
        outs[-1].start()

    def save(layer, *names):
        for name in names:
            out(kept[name].at[layer], saved_out[name].at[layer], save_sem.at[layer, SAVED.index(name)])

    def wide(layer, start, size):
        cols = lanes(start, size)
        return jnp.concatenate([w1[layer, r, place_of(zb, z), :, cols] for r in range(2) for zb in range(RING)], 0)

    def place_gains():
        total = nz[0]
        for i in range(1, 8):
            total = total + nz[i]
        for layer in range(LAYERS):
            for kind in range(4):
                for k in range(6):
                    at = 25 * layer + 6 * kind + k
                    gains[layer, kind : kind + 1, 128 * k : 128 * k + 128] = total[at : at + 1, :]
            pair = total[25 * layer + 24 : 25 * layer + 25, :]
            turned = pltpu.roll(pair, HD, 1)
            first = first_half(1)
            for kind, both in ((4, jnp.where(first, pair, turned)), (5, jnp.where(first, turned, pair))):
                for k in range(6):
                    gains[layer, kind : kind + 1, 128 * k : 128 * k + 128] = both
            gains[layer, 6:8, :] = jnp.zeros((2, D), F32)

    def forward(layer):
        source = tokens if layer == 0 else stream
        moves.complete(3 * layer)
        out(w1.at[layer, :, :, :, 0 : 4 * D], w1_out.at[layer, :, :, :, 0 : 4 * D], out_sem.at[layer, 0])
        if layer == 0:
            place_gains()
        gain_one, bias_one, gain_two, bias_two, gain_query, gain_key = gain_rows(gains, layer)
        norm_into(normed.at[layer], source, gain_one, bias_one)
        for part in range(3):
            joined = dot(normed[layer], wide(layer, D * part, D))
            if part < 2:
                raw[part] = joined
            else:
                values[layer] = joined.astype(BF)
            moves.nudge()
        save(layer, "normed", "values")
        pair_gains = (gain_query[:, 0:128], gain_key[:, 0:128])
        spread = spread_matrix()
        first_one = first_half(128)

        def attend(p):
            at = pl.ds(p * 128, 128)
            low_parts = []
            for part in range(2):
                whole = raw[part, :, at]
                center = whole - head_mean(whole, spread)
                scale = lax.rsqrt(head_mean(center * center, spread) + eps)
                normal = center * scale
                unit[layer, part, :, at] = normal
                scales[layer, part, :, at] = scale.astype(BF)
                low_parts.append((normal * pair_gains[part]).astype(BF))
            queries, keys = low_parts
            for r in range(2):
                rows = slice(128 * r, 128 * r + 128)
                both = split_heads(queries[rows], first_one)
                scores = dot(both, keys[rows], NT) * HD ** (-0.5)
                scores = jnp.where(mask[r] > 0.5, scores, -1e30)
                exponent = jnp.exp(scores - jnp.max(scores, -1, keepdims=True))
                probability = exponent * (1.0 / jnp.sum(exponent, -1, keepdims=True))
                probs[layer, r, p] = probability
                result = dot(probability.astype(BF), values[layer, rows, at])
                mixed[layer, rows, at] = join_heads(result, first_one).astype(BF)

        for p in range(PAIRS):
            attend(p)
            if p % 2:
                moves.nudge()
        save(layer, "unit", "scales", "probs", "mixed")
        middle[layer] = source[...].astype(F32) + dot(mixed[layer], wide(layer, 3 * D, D))
        norm_into(second.at[layer], middle.at[layer], gain_two, bias_two)
        save(layer, "middle", "second")
        moves.nudge()

        def fourth(t):
            cols = lanes(FOURTH * t, FOURTH)
            raw[0] = dot(second[layer], wide(layer, 4 * D + FOURTH * t, FOURTH))

            def activate(r, carry):
                value, derivative = gelu_and_slope(raw[0, r, :])
                hidden[layer, r, cols] = value.astype(BF)
                slope[layer, r, cols] = derivative.astype(BF)
                return carry

            by_rows(activate)

        moves.complete(3 * layer + 1)
        out(w1.at[layer, :, :, :, 4 * D : 8 * D], w1_out.at[layer, :, :, :, 4 * D : 8 * D], out_sem.at[layer, 3])
        for t in range(4):
            fourth(t)
            moves.nudge()
        save(layer, "hidden", "slope")
        moves.complete(3 * layer + 2)
        for zb in range(RING):
            pltpu.make_async_copy(
                wd.at[layer, :, place_of(zb, z)], wd_out.at[layer, :, zb], out_sem.at[layer, 1]
            ).start()
        outs.append(pltpu.make_async_copy(wd.at[layer], wd_out.at[layer], out_sem.at[layer, 1]))
        whole = jnp.concatenate([wd[layer, r, place_of(zb, z)] for r in range(2) for zb in range(RING)], 0)
        result = middle[layer] + dot(hidden[layer], whole)
        if layer + 1 < LAYERS:
            stream[...] = result
            out(stream, stream_out, out_sem.at[layer, 2])
        else:
            act[...] = result.astype(BF)

    for layer in range(LAYERS):
        forward(layer)
    for copy in outs:
        copy.wait()
    net.finish()


def saved_shapes():
    pair = (2, ROWS, D)
    shapes = {
        "normed": ((ROWS, D), BF), "unit": (pair, F32), "scales": (pair, BF), "values": ((ROWS, D), BF),
        "probs": ((2, PAIRS, 256, 128), F32), "mixed": ((ROWS, D), BF), "middle": ((ROWS, D), F32),
        "second": ((ROWS, D), BF), "hidden": ((ROWS, FF), BF), "slope": ((ROWS, FF), BF),
    }
    return [shapes[name] for name in SAVED]


def forward_pass(qkv, out, up, down, norms, tokens, lengths):
    any_spec, vmem_spec = pl.BlockSpec(memory_space=pl.ANY), pl.BlockSpec(memory_space=pltpu.VMEM)
    smem_spec = pl.BlockSpec(memory_space=pltpu.SMEM)
    saved = [((LAYERS, *shape), kind) for shape, kind in saved_shapes()]
    outs = pl.pallas_call(
        forward_kernel,
        out_shape=(
            jax.ShapeDtypeStruct((ROWS, D), BF),
            jax.ShapeDtypeStruct((LAYERS, 2, RING, BLOCK, WIDE), BF),
            jax.ShapeDtypeStruct((LAYERS, 2, RING, DBLOCK, D), BF),
            jax.ShapeDtypeStruct((LAYERS, 8, D), F32),
            jax.ShapeDtypeStruct((ROWS, D), F32),
            *[jax.ShapeDtypeStruct(*item) for item in saved],
        ),
        in_specs=[any_spec, any_spec, any_spec, vmem_spec, vmem_spec, vmem_spec, smem_spec],
        out_specs=(vmem_spec, any_spec, any_spec, vmem_spec, any_spec, *[any_spec] * len(saved)),
        scratch_shapes=[
            *[pltpu.VMEM(*item) for item in saved],
            pltpu.VMEM((LAYERS, 2, RING, BLOCK, WIDE), BF),
            pltpu.VMEM((LAYERS, 2, RING, DBLOCK, D), BF),
            pltpu.VMEM((2, LAYERS, BLOCK, HALF), F32),
            pltpu.VMEM((ROWS, D), F32),
            pltpu.VMEM((2, 256, 128), F32),
            pltpu.VMEM((2, ROWS, D), F32),
            pltpu.VMEM((8, 256), F32),
            pltpu.VMEM((2, 56, 128), F32),
            pltpu.VMEM((2, 56, 128), F32),
            pltpu.VMEM((8, 56, 128), F32),
            pltpu.SemaphoreType.DMA((GATHER_COPIES,)),
            pltpu.SemaphoreType.DMA((GATHER_COPIES,)),
            pltpu.SemaphoreType.DMA((2,)),
            pltpu.SemaphoreType.DMA((LAYERS, 4)),
            pltpu.SemaphoreType.DMA((LAYERS, len(SAVED))),
        ],
        compiler_params=pltpu.CompilerParams(
            collective_id=0, has_side_effects=True, vmem_limit_bytes=63 * 1024 * 1024
        ),
        name="gather_and_forward",
    )(qkv, out, up, down, norms, tokens, lengths)
    return outs[0], outs[1], outs[2], outs[3], outs[4], outs[5:]


HALVES = (slice(4, 8), slice(0, 4))
PARTS = tuple((slice(7 - i, 8 - i), slice(i, i + 1)) for i in range(4))
SCATTER_COPIES = 150
SUM_ORDER = tuple((layer, kind) for layer in (1, 0) for kind in ("down", "up", "qkvo"))


class Scatter:
    def __init__(self, me, net, grads, buffers, sems):
        self.me, self.net, self.grads, self.b = me, net, grads, buffers
        self.local, self.swap_send, self.swap_recv, self.credit = sems
        self.sibling, self.xs, self.ys, self.zs = me.neighbours()
        self.chunks = [self.chunk(i, layer, kind) for i, (layer, kind) in enumerate(SUM_ORDER)]
        self.kept, self.swapped, self.turns = [], [], 0

    def chunk(self, index, layer, kind):
        me, b, down = self.me, self.b, kind == "down"
        own = b["own_" + kind]

        def q(at, k):
            if down:
                return own.at[layer, :, at, rows16(16 * k, 16), :]
            return own.at[layer, :, at, :, lanes(QUARTER * k, QUARTER)]

        def p(at, k):
            if down:
                return own.at[layer, k[0], at, rows16(64 + 16 * k[1], 16), :]
            return own.at[layer, k[0], at, :, lanes(C_START + C_WIDTH * k[1], C_WIDTH)]

        def a(at):
            return own.at[layer, :, at, :, A_START : A_START + A_WIDTH]

        def q_buffer(name):
            return lambda at: b[name + kind].at[layer, :, at]

        def p_buffer(name):
            return lambda at: b[name + kind].at[layer, at]

        def z_pair(name):
            return {1: (b["zp" + name + kind], layer), -1: (b["zm" + name + kind], layer)}

        fours = [
            (q, me.on_y, self.ys, *[q_buffer(name) for name in ("yf_", "yp_", "ym_")]),
            (p, me.on_x, self.xs, *[p_buffer(name) for name in ("xf_", "xp_", "xm_")]),
        ]
        long = 1 if kind == "up" else -1
        chain = [
            (lambda at: q(at, me.y), long, z_pair("q_")),
            (lambda at: p(at, me.on_x(0)), -long, z_pair("p_")),
        ]
        spare = [] if down else [(a, 1, z_pair("a_"))]
        return SimpleNamespace(
            index=index, layer=layer, kind=kind, fours=fours, chain=chain, spare=spare,
            far={}, second={}, near=None, moving=None, aside=None, at=0, ready=False,
        )

    def mine_and_theirs(self, chunk):
        return self.b["own_" + chunk.kind].at[chunk.layer], self.b["sib_" + chunk.kind]

    def swap_copy(self, chunk, src, dst):
        i = chunk.index
        return pltpu.make_async_remote_copy(
            src, dst, self.swap_send.at[i], self.swap_recv.at[i], device_id=self.sibling, device_id_type=MESH
        )

    def load(self, chunk):
        layer, c, kind = chunk.layer, self.me.c, chunk.kind
        mine, theirs = self.mine_and_theirs(chunk)
        sem = self.local.at[chunk.index]
        if kind != "qkvo":
            grad = self.grads[kind][layer]

            def half(core):
                if kind == "down":
                    return grad.at[:, :, rows16(96 * core, 96), :]
                return grad.at[:, :, :, lanes(HALF * core, HALF)]

            pltpu.make_async_copy(half(c), mine, sem).start()
            self.swap_copy(chunk, half(1 - c), theirs).start()
            return
        qkv, out = (self.grads[name][layer] for name in ("qkv", "out"))

        def parts(core, to):
            if core == 0:
                return [(qkv.at[:, :, :, 0:HALF], to)]
            return [(qkv.at[:, :, :, HALF : 3 * D], to.at[:, :, :, 0:D]), (out, to.at[:, :, :, D:HALF])]

        for core in range(2):

            @pl.when(c == core)
            def _():
                for src, dst in parts(core, mine):
                    pltpu.make_async_copy(src, dst, sem).start()
                for src, dst in parts(1 - core, theirs):
                    self.swap_copy(chunk, src, dst).start()

    def loaded(self, chunk):
        mine, theirs = self.mine_and_theirs(chunk)
        pltpu.make_async_copy(mine, mine, self.local.at[chunk.index]).wait()
        self.swap_copy(chunk, mine, theirs).wait_recv()

        def add(i, carry):
            for rows in range(2):
                mine[rows, i] = mine[rows, i] + theirs[rows, i]
            return carry

        lax.fori_loop(0, RING, add, 0)

    @staticmethod
    def sum_into(ref, *others):
        total = ref[...]
        for other in others:
            total = total + other[...]
        ref[...] = total

    def four_far(self, chunk, part):
        chunk.far[part] = self.net.batch()
        for d, at in zip((1, -1), PARTS[part]):
            for view, k, devices, first, ahead, behind in chunk.fours:
                chunk.far[part].put(view(at, k(2)), first(at), devices[d])

    def four_near(self, chunk):
        chunk.near = self.net.batch()
        for d, at in zip((1, -1), HALVES):
            for view, k, devices, first, ahead, behind in chunk.fours:
                back = ahead if d == -1 else behind
                chunk.near.put(view(at, k(-d)), back(at), devices[-d])

    def four_second(self, chunk, part):
        chunk.far[part].wait_recv()
        chunk.second[part] = self.net.batch()
        for d, at in zip((1, -1), PARTS[part]):
            for view, k, devices, first, ahead, behind in chunk.fours:
                block, front = view(at, k(d)), ahead if d == 1 else behind
                self.sum_into(block, first(at))
                chunk.second[part].put(block, front(at), devices[d])

    def four_last(self, chunk, part):
        if part == 0:
            chunk.near.wait_recv()
        chunk.second[part].wait_recv()
        for at in PARTS[part]:
            for view, k, devices, first, ahead, behind in chunk.fours:
                self.sum_into(view(at, k(0)), ahead(at), behind(at))

    def chain_step(self, pieces, k, before):
        if before:
            before.wait_recv()
        batch = self.net.batch()
        for view, long, buffers in pieces:
            for d in (1, -1):
                if k == 1 and d != long:
                    continue
                block = view(PLACES[d * (5 - k)])
                buffer, layer = buffers[d]
                if k > 2 or k == 2 and d == long:
                    self.sum_into(block, buffer.at[k - 2, layer])
                batch.put(block, buffer.at[k - 1, layer], self.zs[d])
        return batch

    def chain_last(self, pieces, before):
        before.wait_recv()
        for view, long, buffers in pieces:
            self.sum_into(view(PLACES[0]), *[buffers[d][0].at[3, buffers[d][1]] for d in (1, -1)])

    def begin(self, i):
        chunk = self.chunks[i]
        if chunk.layer == 0:
            while self.chunks[i - 3].at < 1:
                self.tick(self.chunks[i - 3])
            pl.semaphore_wait(self.credit.at[KINDS.index(chunk.kind)], 1)
        self.load(chunk)
        chunk.ready, chunk.begun = True, self.turns

    def tick(self, chunk):
        t = chunk.at
        chunk.at += 1
        if t > 6:
            self.to_copies(chunk) if t == 7 else self.to_sibling(chunk)
            return
        if t == 0:
            self.loaded(chunk)
            if chunk.layer == 1:
                pl.semaphore_signal(
                    self.credit.at[KINDS.index(chunk.kind)], inc=1, device_id=self.sibling, device_id_type=MESH
                )
        if t < 4:
            self.four_far(chunk, t)
        if t == 0:
            self.four_near(chunk)
        if 1 <= t <= 4:
            self.four_second(chunk, t - 1)
        if 2 <= t <= 5:
            self.four_last(chunk, t - 2)
        if 2 <= t < 6:
            chunk.moving = self.chain_step(chunk.chain, t - 1, chunk.moving)
        if t < 4 and chunk.spare:
            chunk.aside = self.chain_step(chunk.spare, t + 1, chunk.aside)
        if t == 6:
            if chunk.spare:
                self.chain_last(chunk.spare, chunk.aside)
            self.chain_last(chunk.chain, chunk.moving)
            self.over_copies(chunk)

    def slots(self, chunk, name):
        return self.b[name + chunk.kind].at[chunk.layer]

    @staticmethod
    def sum_slots(slots):
        total = slots[0].astype(F32)
        for i in range(1, 4):
            total = total + slots[i].astype(F32)
        return total.astype(BF)

    def over_copies(self, chunk):
        me, net, layer, down = self.me, self.net, chunk.layer, chunk.kind == "down"
        x, y, z, xl, xh = me.x, me.y, PLACES[0], me.xl, me.xh
        own = self.b["own_" + chunk.kind]

        def part_q(k):
            if down:
                return own.at[layer, k, z, rows16(16 * y, 16), :]
            return own.at[layer, k, z, :, lanes(QUARTER * y, QUARTER)]

        def part_a(k):
            return own.at[layer, k, z, :, A_START : A_START + A_WIDTH]

        over_x, over_y = net.batch(), net.batch()
        for view, name in ((part_q, "xs_"), (part_a, "xa_"))[: 1 if down else 2]:
            slots = self.slots(chunk, name)
            for d in (1, -1, 2):
                over_x.put(view(xl if d == 2 else 1 - xl), slots.at[x], self.xs[d])
            slots[x] = view(xl)[...]
        if down:
            part_p = own.at[layer, xl, z, rows16(64 + 16 * xh, 16), :]
        else:
            part_p = own.at[layer, xl, z, :, lanes(C_START + C_WIDTH * xh, C_WIDTH)]
        slots = self.slots(chunk, "ys_")
        for d in (1, -1, 2):
            over_y.put(part_p, slots.at[y], self.ys[d])
        slots[y] = part_p[...]
        chunk.over = (over_x, over_y)

    def to_copies(self, chunk):
        me, net, down = self.me, self.net, chunk.kind == "down"
        x, y, xh = me.x, me.y, me.xh
        total = self.b["out_down" if down else "rb_" + chunk.kind].at[chunk.layer]
        over_x, over_y = chunk.over
        last = net.batch()
        over_x.wait_recv()
        if not down:
            slots = self.slots(chunk, "ya_")
            slots[y] = self.sum_slots(self.slots(chunk, "xa_"))
            for d in (1, -1, 2):
                last.put(slots.at[y], slots.at[y], self.ys[d])
        mine = total.at[rows16(16 * y, 16), :] if down else total.at[:, lanes(QUARTER * y, QUARTER)]
        mine[...] = self.sum_slots(self.slots(chunk, "xs_"))
        for d in (1, -1, 2):
            last.put(mine, mine, self.ys[d])
        over_y.wait_recv()
        if down:
            mine = total.at[rows16(64 + 16 * xh, 16), :]
        else:
            mine = total.at[:, lanes(C_START + C_WIDTH * xh, C_WIDTH)]
        mine[...] = self.sum_slots(self.slots(chunk, "ys_"))
        last.put(mine, mine, self.xs[2])
        chunk.last = last

    def to_sibling(self, chunk):
        chunk.last.wait_recv()
        kind, layer, c = chunk.kind, chunk.layer, self.me.c
        if kind == "down":
            return
        total, wide = self.b["rb_" + kind].at[layer], self.b["rf_" + kind].at[layer]
        total[:, A_START : A_START + A_WIDTH] = self.sum_slots(self.slots(chunk, "ya_"))
        wide[...] = total[...].astype(F32)
        target = self.b["out_wide"].at[layer, :, lanes(STARTS[kind] + c * HALF, HALF)]
        self.swapped.append(self.net.put(wide.at[pl.ds(24 * (1 - c), 24), :], target, self.sibling))
        keep = pltpu.make_async_copy(wide.at[pl.ds(24 * c, 24), :], target, self.local.at[6 + len(self.kept)])
        keep.start()
        self.kept.append(keep)

    def turn(self, rest=None):
        self.turns += 1
        rest = GAP if rest is None else rest
        open_chunks = [ch for ch in self.chunks if ch.ready and ch.at < 9]
        rested = [ch for ch in open_chunks if self.turns - ch.begun >= (rest if ch.at else rest and REST)]
        for chunk in sorted(rested, key=lambda ch: SUM_AFTER[ch.index] + ch.at)[:AT_ONCE]:
            chunk.begun = self.turns
            self.tick(chunk)
        return bool(open_chunks)

    def swaps_sent(self):
        for chunk in self.chunks:
            self.swap_copy(chunk, *self.mine_and_theirs(chunk)).wait_send()


SUM_AFTER = (0, 2, 4, 6, 8, 10)
REST = 4
GAP = 3
AT_ONCE = 5


def buffer_shapes():
    shapes = {}
    for kind in KINDS:
        rows, cols = (96, D) if kind == "down" else (BLOCK, HALF)
        quarter = (16, D) if kind == "down" else (BLOCK, QUARTER)
        half = (16, D) if kind == "down" else (BLOCK, C_WIDTH)
        shapes["own_" + kind] = (2, 2, RING, rows, cols)
        shapes["sib_" + kind] = (2, RING, rows, cols)
        for name in ("yf_", "yp_", "ym_"):
            shapes[name + kind] = (2, 2, RING, *quarter)
        for name in ("xf_", "xp_", "xm_"):
            shapes[name + kind] = (2, RING, *half)
        for name in ("zp", "zm"):
            shapes[name + "q_" + kind] = (4, 2, 2, *quarter)
            shapes[name + "p_" + kind] = (4, 2, *half)
        shapes["xs_" + kind] = (2, 4, *quarter)
        shapes["ys_" + kind] = (2, 4, *half)
        if kind != "down":
            for name in ("zp", "zm"):
                shapes[name + "a_" + kind] = (4, 2, 2, BLOCK, A_WIDTH)
            shapes["xa_" + kind] = shapes["ya_" + kind] = (2, 4, BLOCK, A_WIDTH)
            shapes["rb_" + kind] = (2, BLOCK, HALF)
    return shapes


BUFFERS = buffer_shapes()
WEIGHT_SLOTS = 3
STAGE_SLOTS = 2
GRAD_SHAPES = {"qkv": (D, 3 * D), "out": (D, D), "up": (D, FF), "down": (FF, D)}


def backward_kernel(tokens, cotangent, gains, w1_ref, wd_ref, stream_ref, *rest):
    saved, rest = dict(zip(SAVED, rest)), rest[len(SAVED) :]
    input_grad, out1, outd, outn = rest[:4]
    grads_flat, rest = rest[4:12], rest[12:]
    names = tuple(GRAD_SHAPES)
    grads = {name: grads_flat[2 * i : 2 * i + 2] for i, name in enumerate(names)}
    kept, rest = dict(zip(SAVED, rest)), rest[len(SAVED) :]
    b, rest = dict(zip(BUFFERS, rest)), rest[len(BUFFERS) :]
    (
        rf, stream, weight, low, wide_low, grad, slow, turned, stage, gn, norm_sum, nc, nz, ny, nx,
        send, recv, local, swap_send, swap_recv, credit, load_sem, weight_sem, store_sem, plain_sem,
    ) = rest
    unit, scales, values, probs = (kept[name] for name in ("unit", "scales", "values", "probs"))
    me = Place()
    x, y, z, c, xl, xh = me.x, me.y, me.z, me.c, me.xl, me.xh
    sibling, xs, ys, zs = me.neighbours()

    met = greet([sibling, *xs.values(), *ys.values(), *zs.values()])
    use_order = ("hidden", "slope", "second", "middle", "mixed", "probs", "values", "unit", "scales", "normed")
    fetched = {}

    def fetch(layer, *wanted):
        for name in wanted:
            fetched[name] = pltpu.make_async_copy(
                saved[name].at[layer], kept[name], load_sem.at[SAVED.index(name)]
            )
            fetched[name].start()

    wide_weight = weight.reshape(WEIGHT_SLOTS, 2, RING, BLOCK, D)
    tall_weight = weight.reshape(WEIGHT_SLOTS, 4, DBLOCK, D)
    weight_views = []
    for layer in reversed(range(LAYERS)):
        for t in range(4):
            weight_views.append((wd_ref.at[layer, t // 2, t % 2 * 4 : t % 2 * 4 + 4], tall_weight))
        for start in (*[4 * D + FOURTH * t for t in range(4)], 3 * D, 0, D, 2 * D):
            weight_views.append((w1_ref.at[layer, :, :, :, start : start + D], wide_weight))
    weight_copies = []

    def ask_weight():
        n = len(weight_copies)
        if n < len(weight_views):
            slot = n % WEIGHT_SLOTS
            view, to = weight_views[n]
            weight_copies.append(pltpu.make_async_copy(view, to.at[slot], weight_sem.at[slot]))
            weight_copies[-1].start()

    taken = []

    def take_weight():
        n = len(taken)
        taken.append(n)
        weight_copies[n].wait()
        slot = n % WEIGHT_SLOTS
        if weight_views[n][1] is tall_weight:
            return weight[slot]
        return jnp.concatenate(
            [wide_weight[slot, r, place_of(zb, z)] for r in range(2) for zb in range(RING)], 0
        )

    first_copies = [
        pltpu.make_async_copy(cotangent, low, plain_sem.at[0]),
        pltpu.make_async_copy(stream_ref, stream, plain_sem.at[1]),
    ]
    first_copies[0].start()
    ask_weight()
    fetch(1, *use_order[:2])
    for i in range(WEIGHT_SLOTS - 1):
        ask_weight()
    fetch(1, *use_order[2:])
    first_copies[1].start()

    net = Net(send, recv, sibling, b["own_qkvo"].at[0, 0])
    shaped = {name: grads[name] for name in names}
    b.update(out_down=outd, out_wide=out1, rf_qkvo=rf.at[0], rf_up=rf.at[1])
    sums = Scatter(me, net, shaped, b, (local, swap_send, swap_recv, credit))

    pending = {}
    count = [0]

    def flush():
        for copy in pending.values():
            copy.wait()
        pending.clear()

    def emit(value, name, layer, start, by_row):
        slot = count[0] % STAGE_SLOTS
        count[0] += 1
        if slot in pending:
            pending.pop(slot).wait()
        target, low_value = grads[name][layer], value.astype(BF)
        whole = stage.at[slot]
        if by_row:
            stage[slot] = low_value
            for i in range(4):
                row = start // DBLOCK + i
                pltpu.make_async_copy(
                    stage.at[slot, DBLOCK * i : DBLOCK * i + DBLOCK],
                    target.at[row // RING, place_of(row % RING, z)],
                    store_sem.at[slot],
                ).start()
            pending[slot] = pltpu.make_async_copy(whole, whole, store_sem.at[slot])
            return
        src = stage.at[slot].reshape(2, RING, BLOCK, D)
        for row in range(2 * RING):
            src[row // RING, place_of(row % RING, z)] = low_value[BLOCK * row : BLOCK * row + BLOCK]
        pending[slot] = pltpu.make_async_copy(src, target.at[:, :, :, start : start + D], store_sem.at[slot])
        pending[slot].start()

    def put_rows(layer, kind, rows):
        for i, row in enumerate(rows):
            for k in range(6):
                at = 25 * layer + 6 * (kind + i) + k
                gn[at : at + 1, :] = row[:, 128 * k : 128 * k + 128]

    def backward(layer):
        again = layer > 0
        gain_one, bias_one, gain_two, bias_two, gain_query, gain_key = gain_rows(gains, layer)
        slope, hidden = kept["slope"], kept["hidden"]
        fetched["hidden"].wait()
        fetched["slope"].wait()
        for t in range(4):
            cols = slice(FOURTH * t, FOURTH * t + FOURTH)
            grad_hidden = dot(low[...], take_weight(), NT)
            wide_low[:, cols] = (slope[:, cols].astype(F32) * grad_hidden).astype(BF)
            ask_weight()
            turned[...] = hidden[:, cols].T
            emit(dot(turned[...], low[...]), "down", layer, FOURTH * t, True)
            sums.turn()
        fetched["second"].wait()
        turned[...] = kept["second"][...].T
        if again:
            fetch(layer - 1, "slope", "hidden", "second")
        for t in range(4):
            cols = slice(FOURTH * t, FOURTH * t + FOURTH)
            part = dot(wide_low[:, cols], take_weight(), NT)
            slow[...] = part if t == 0 else slow[...] + part
            ask_weight()
            if t == 0:
                flush()
                if layer == 1:
                    met()
                sums.begin(0 if layer == 1 else 3)
            emit(dot(turned[...], wide_low[:, cols]), "up", layer, FOURTH * t, False)
            sums.turn()
        flush()
        sums.begin(1 if layer == 1 else 4)
        fetched["middle"].wait()
        put_rows(layer, 2, norm_back(kept["middle"], slow, gain_two, grad, low))
        fetched["mixed"].wait()
        turned[...] = kept["mixed"][...].T
        if again:
            fetch(layer - 1, "middle", "mixed")
        emit(dot(turned[...], low[...]), "out", layer, 0, False)
        wide_low[:, 3 * D : 4 * D] = dot(low[...], take_weight(), NT).astype(BF)
        ask_weight()
        sums.turn()
        for name in ("probs", "values", "unit", "scales"):
            fetched[name].wait()
        pair_gains = (gain_query[:, 0:128], gain_key[:, 0:128])
        spread = spread_matrix()
        first_one = first_half(128)

        def attend(p, carry):
            at = pl.ds(p * 128, 128)
            normals = [unit[part, :, at] for part in range(2)]
            queries, keys = ((normals[part] * pair_gains[part]).astype(BF) for part in range(2))
            slopes = ([], [])
            for r in range(2):
                rows = slice(128 * r, 128 * r + 128)
                both = split_heads(queries[rows], first_one)
                grad_both = split_heads(wide_low[rows, pl.ds(3 * D + p * 128, 128)], first_one)
                probability = probs[r, p]
                grad_values = dot(probability.astype(BF), grad_both, TN)
                wide_low[rows, pl.ds(2 * D + p * 128, 128)] = grad_values.astype(BF)
                grad_probs = dot(grad_both, values[rows, at], NT)
                weighted = grad_probs * probability
                inner = jnp.sum(weighted, -1, keepdims=True)
                grad_scores = (weighted - probability * inner).astype(BF)
                slopes[0].append(join_heads(dot(grad_scores, keys[rows]), first_one) * HD ** (-0.5))
                slopes[1].append(dot(grad_scores, both, TN) * HD ** (-0.5))
            sums_now = []
            for part in range(2):
                up = jnp.concatenate(slopes[part], 0)
                normal = normals[part]
                sums_now.append(carry[part] + fold(up * normal))
                inner = up * pair_gains[part]
                along = head_mean(inner * normal, spread)
                result = scales[part, :, at].astype(F32) * (inner - head_mean(inner, spread) - normal * along)
                wide_low[:, pl.ds(part * D + p * 128, 128)] = result.astype(BF)
            return tuple(sums_now)

        zero = jnp.zeros((8, 128), F32)
        head_sums = (zero, zero)
        for p in range(PAIRS):
            head_sums = attend(p, head_sums)
            if p % 2:
                sums.turn()
        totals = []
        for part in head_sums:
            total = jnp.sum(part, 0, keepdims=True)
            totals.append(total + pltpu.roll(total, HD, 1))
        gn[25 * layer + 24 : 25 * layer + 25, :] = jnp.where(first_half(1), *totals)
        if again:
            fetch(layer - 1, "probs", "values", "unit", "scales")
        fetched["normed"].wait()
        turned[...] = kept["normed"][...].T
        if again:
            fetch(layer - 1, "normed")
        for part in range(3):
            cols = slice(D * part, D * part + D)
            emit(dot(turned[...], wide_low[:, cols]), "qkv", layer, D * part, False)
            sums.turn()
        flush()
        sums.begin(2 if layer == 1 else 5)
        for part in range(3):
            cols = slice(D * part, D * part + D)
            piece = dot(wide_low[:, cols], take_weight(), NT)
            slow[...] = piece if part == 0 else slow[...] + piece
            ask_weight()
        if layer == 1:
            first_copies[1].wait()
        put_rows(layer, 0, norm_back(stream if layer == 1 else tokens, slow, gain_one, grad, low))

    first_copies[0].wait()

    def turn(r, carry):
        grad[r, :] = low[r, :].astype(F32)
        return carry

    by_rows(turn)
    gn[...] = jnp.zeros(gn.shape, F32)
    for layer in reversed(range(LAYERS)):
        backward(layer)
    grad_out = pltpu.make_async_copy(low, input_grad, plain_sem.at[0])
    grad_out.start()

    nc[c] = gn[...]
    norm_swap = net.put(gn, nc.at[c], sibling)
    norm_moving = [norm_swap]

    def norm_ring(k):
        copies = []
        for d in (1, -1):
            if k < 4 or d == 1:
                slot = nz.at[(z - d * (k - 1) + 8) % 8]
                copies.append(net.put(slot, slot, zs[d]))
        return copies

    t = 0
    while sums.turn(0) or t < 7:
        if sums.chunks[-2].at > 8:
            net.settle(20)
        arrive(norm_moving)
        norm_moving = []
        if t == 0:
            nz[z] = nc[0] + nc[1]
        if t < 4:
            norm_moving = norm_ring(t + 1)
        elif t == 4:
            total = nz[0]
            for i in range(1, 8):
                total = total + nz[i]
            ny[y] = total
            norm_moving = [net.put(ny.at[y], ny.at[y], ys[d]) for d in (1, -1, 2)]
        elif t == 5:
            nx[x] = ny[0] + ny[1] + ny[2] + ny[3]
            norm_moving = [net.put(nx.at[x], nx.at[x], xs[d]) for d in (1, -1, 2)]
        elif t == 6:
            norm_sum[0:56, :] = nx[0] + nx[1] + nx[2] + nx[3]
        t += 1

    arrive(sums.swapped)
    shard = lax.axis_index("shard")
    for row, (layer, first) in enumerate(((0, 100 * shard), (1, 100 * shard), (0, 3 * D + 24 * shard), (1, 3 * D + 24 * shard))):
        at = 25 * layer + first // 128
        pair = [jnp.broadcast_to(norm_sum[pl.ds(at + i, 1), :], (8, 128)) for i in range(2)]
        turned_row = pltpu.roll(jnp.concatenate(pair, 1), (256 - first % 128) % 256, 1)
        outn[row : row + 1, :] = turned_row[0:1, 0:128]
    outn[4:8, :] = jnp.zeros((4, 128), F32)
    for copy in sums.kept:
        copy.wait()
    grad_out.wait()
    net.finish()
    sums.swaps_sent()


def backward_pass(tokens, cotangent, gains, w1, wd, stream, saved):
    any_spec, vmem_spec = pl.BlockSpec(memory_space=pl.ANY), pl.BlockSpec(memory_space=pltpu.VMEM)
    grad_shapes = [
        (2, RING, shape[0] // 16, shape[1]) for shape in GRAD_SHAPES.values() for layer in range(LAYERS)
    ]
    outs = pl.pallas_call(
        backward_kernel,
        out_shape=(
            jax.ShapeDtypeStruct((ROWS, D), BF),
            jax.ShapeDtypeStruct((LAYERS, 24, WIDE), F32),
            jax.ShapeDtypeStruct((LAYERS, 96, D), BF),
            jax.ShapeDtypeStruct((8, 128), F32),
            *[jax.ShapeDtypeStruct(shape, BF) for shape in grad_shapes],
        ),
        in_specs=[vmem_spec, any_spec, vmem_spec, any_spec, any_spec, any_spec, *[any_spec] * len(SAVED)],
        out_specs=(any_spec, any_spec, vmem_spec, vmem_spec, *[any_spec] * len(grad_shapes)),
        scratch_shapes=[
            *[pltpu.VMEM(*item) for item in saved_shapes()],
            *[pltpu.VMEM(shape, BF) for shape in BUFFERS.values()],
            pltpu.VMEM((2, 2, BLOCK, HALF), F32),
            pltpu.VMEM((ROWS, D), F32),
            pltpu.VMEM((WEIGHT_SLOTS, D, D), BF),
            pltpu.VMEM((ROWS, D), BF),
            pltpu.VMEM((ROWS, FF), BF),
            pltpu.VMEM((ROWS, D), F32),
            pltpu.VMEM((ROWS, D), F32),
            pltpu.VMEM((D, ROWS), BF),
            pltpu.VMEM((STAGE_SLOTS, D, D), BF),
            pltpu.VMEM((56, 128), F32),
            pltpu.VMEM((64, 128), F32),
            pltpu.VMEM((2, 56, 128), F32),
            pltpu.VMEM((8, 56, 128), F32),
            pltpu.VMEM((4, 56, 128), F32),
            pltpu.VMEM((4, 56, 128), F32),
            pltpu.SemaphoreType.DMA((SCATTER_COPIES,)),
            pltpu.SemaphoreType.DMA((SCATTER_COPIES,)),
            pltpu.SemaphoreType.DMA((10,)),
            pltpu.SemaphoreType.DMA((6,)),
            pltpu.SemaphoreType.DMA((6,)),
            pltpu.SemaphoreType.REGULAR((3,)),
            pltpu.SemaphoreType.DMA((len(SAVED),)),
            pltpu.SemaphoreType.DMA((WEIGHT_SLOTS,)),
            pltpu.SemaphoreType.DMA((STAGE_SLOTS,)),
            pltpu.SemaphoreType.DMA((2,)),
        ],
        compiler_params=pltpu.CompilerParams(
            collective_id=1, has_side_effects=True, vmem_limit_bytes=63 * 1024 * 1024
        ),
        name="backward_and_scatter",
    )(tokens, cotangent, gains, w1, wd, stream, *saved)
    return outs[:4]


STEPS = 3
FACTOR = 65536 ** (-0.5)


def updated(gradient_sum, master, moment, average):
    gradient_scaled = gradient_sum * FACTOR
    moment_new = momentum_decay * moment + gradient_scaled
    master_new = master - learn_rate * (gradient_scaled + momentum_decay * moment_new)
    average_new = average_decay * average + (1.0 - average_decay) * master_new
    return master_new, moment_new, average_new, master_new.astype(BF)


def update_kernel(*refs):
    ins, outs = refs[:22], refs[22:]
    for i in range(5):
        sums, old, new = ins[4 * i], ins[4 * i + 1 : 4 * i + 4], outs[4 * i : 4 * i + 4]
        total = sums[0:2, 0:100] if i == 4 else sums[...].astype(F32)
        for ref, value in zip(new, updated(total, *[ref[...] for ref in old])):
            ref[...] = value
    for i in range(2):
        outs[20 + i][...] = ins[20 + i][...]
    outs[22][...] = ins[16][2:4, 0:24] * FACTOR


def update(sums, states, rows):
    in_specs, out_specs, shapes, args = [], [], [], []
    starts = (0, 3 * D, 4 * D, 0, 0)
    for start, total, state in zip(starts, sums, states):
        shape = state[0].shape
        if len(shape) == 2:
            block, place = shape, lambda i: (0, 0)
            total_block, total_place = total.shape, place
        elif shape[1] == 96:
            block, place = (shape[0], shape[1] // STEPS, shape[2]), lambda i: (0, i, 0)
            total_block, total_place = block, place
        else:
            block, place = (*shape[:2], shape[2] // STEPS), lambda i: (0, 0, i)
            total_block, total_place = block, lambda i, first=start // (shape[2] // STEPS): (0, 0, first + i)
        spec = pl.BlockSpec(block, place)
        in_specs += [pl.BlockSpec(total_block, total_place), spec, spec, spec]
        out_specs += [spec] * 4
        shapes += [jax.ShapeDtypeStruct(shape, kind) for kind in (F32, F32, F32, BF)]
        args += [total, *state]
    row_spec = pl.BlockSpec((ROWS, D // STEPS), lambda i: (0, i))
    shift = (LAYERS, 24)
    return pl.pallas_call(
        update_kernel,
        grid=(STEPS,),
        out_shape=[*shapes, *[jax.ShapeDtypeStruct((ROWS, D), BF)] * 2, jax.ShapeDtypeStruct(shift, F32)],
        in_specs=[*in_specs, row_spec, row_spec],
        out_specs=[*out_specs, row_spec, row_spec, pl.BlockSpec(shift, lambda i: (0, 0))],
        compiler_params=pltpu.CompilerParams(vmem_limit_bytes=63 * 1024 * 1024),
        name="update",
    )(*args, *rows)


def body(
    tokens, cotangent, picture_lengths, w_qkv, mom_qkv, ema_qkv, w_out, mom_out, ema_out, w_up, mom_up, ema_up,
    w_down, mom_down, ema_down, norms, mom_norms, ema_norms,
):
    flat_tokens = tokens.reshape(ROWS, D)
    act, w1, wd, gains, stream, saved = forward_pass(
        w_qkv, w_out, w_up, w_down, norms, flat_tokens, picture_lengths.reshape(2, 4)
    )
    input_grad, sum1, sumd, sumn = backward_pass(
        flat_tokens, cotangent.reshape(ROWS, D), gains, w1, wd, stream, saved
    )
    outs = update(
        (sum1, sum1, sum1, sumd, sumn),
        (
            (w_qkv, mom_qkv, ema_qkv), (w_out, mom_out, ema_out), (w_up, mom_up, ema_up),
            (w_down, mom_down, ema_down), (norms, mom_norms, ema_norms),
        ),
        (act, input_grad),
    )
    return (outs[20].reshape(tokens.shape), outs[21].reshape(tokens.shape), *outs[:20], outs[22])


def solution(mesh):
    rows = P(None, ("shard", "rep"), None, None)
    wide, flat = P(None, "shard", None), P(None, "shard")
    return jax.shard_map(
        body,
        mesh=mesh,
        in_specs=(rows, rows, P(None, ("shard", "rep"), None), *[wide] * 12, *[flat] * 3),
        out_specs=(rows, rows, *[wide] * 16, *[flat] * 5),
        check_vma=False,
    )
```

```python
import math
from types import SimpleNamespace

import jax
import jax.numpy as jnp
from jax import lax
from jax.experimental import pallas as pl
from jax.experimental.pallas import tpu as pltpu
from jax.sharding import PartitionSpec as P

D = 768
HEADS = 12
HD = 64
FF = 3072
LAYERS = 2
ROWS = 256
PAIRS = HEADS // 2
CHUNK = 64
FOURTH = 768
RING = 8
BLOCK = 48
DBLOCK = 192
WIDE = 6144
HALF = 1536
QUARTER = 128
C_START, C_WIDTH = 512, 384
A_START, A_WIDTH = 1280, 256
STARTS = {"qkvo": 0, "up": 4 * D}
KINDS = ("qkvo", "up", "down")
PLACES = {off: off + 3 for off in range(-3, 5)} | {-4: 7}
GROUPS = ((3, None), (2, 4), (1, 5), (0, 6), (None, 7))
MESH = pl.DeviceIdType.MESH
BF = jnp.bfloat16
F32 = jnp.float32
NT = (((1,), (1,)), ((), ()))
NN = (((1,), (0,)), ((), ()))
TN = (((0,), (0,)), ((), ()))

eps = 1e-06
momentum_decay = 0.9
average_decay = 0.99
learn_rate = 0.03


class Place:
    def __init__(self):
        shard, rep = lax.axis_index("shard"), lax.axis_index("rep")
        self.c = shard % 2
        self.z = (shard // 2) % 8
        self.xl = shard // 16
        self.xh = rep % 2
        self.y = rep // 2
        self.x = self.xh * 2 + self.xl
        self.ys = [(self.y + d) % 4 for d in range(4)]
        self.xs = [((self.x + d) % 2, (self.x + d) % 4 // 2) for d in range(4)]

    def on_y(self, d):
        return self.ys[d % 4]

    def on_x(self, d):
        return self.xs[d % 4]

    def at(self, x=None, y=None, z=None, c=None):
        x = self.x if x is None else x
        y = self.y if y is None else y
        z = self.z if z is None else z
        c = self.c if c is None else c
        return (((x % 2) * 8 + z) * 2 + c, y * 2 + x // 2)

    def neighbours(self):
        sibling = self.at(c=1 - self.c)
        xs = {d: self.at(x=(self.x + d) % 4) for d in (1, -1, 2)}
        ys = {d: self.at(y=(self.y + d) % 4) for d in (1, -1, 2)}
        zs = {d: self.at(z=(self.z + d) % 8) for d in (1, -1)}
        return sibling, xs, ys, zs


class Net:
    def __init__(self, send, recv, someone, ruler):
        self.send, self.recv, self.someone, self.ruler = send, recv, someone, ruler
        self.count, self.sent = 0, []

    def copy(self, src, dst, device, at):
        return pltpu.make_async_remote_copy(
            src_ref=src,
            dst_ref=dst,
            send_sem=self.send.at[at],
            recv_sem=self.recv.at[at],
            device_id=device,
            device_id_type=MESH,
        )

    def reserve(self):
        self.count += 1
        assert self.count <= self.send.shape[0]
        return self.count - 1

    def put(self, src, dst, device):
        copy = self.copy(src, dst, device, self.reserve())
        copy.start()
        self.sent.append(copy)
        return copy

    def batch(self):
        self.sent.append(Batch(self))
        return self.sent[-1]

    def settle(self, most):
        kept = []
        for copy in self.sent[:most]:
            if isinstance(copy, Batch) and copy.grows:
                kept.append(copy)
            else:
                copy.wait_send()
        self.sent = kept + self.sent[most:]

    def finish(self):
        self.settle(len(self.sent))


class Batch:
    def __init__(self, net):
        self.net, self.at, self.size, self.grows = net, net.reserve(), 0, False

    def put(self, src, dst, device):
        self.net.copy(src, dst, device, self.at).start()
        self.size += math.prod(src.shape)

    def whole(self):
        tiles, ruler = self.size // 2048, self.net.ruler
        for blocks, depth in ((1, 16), (1, 48), (2, 48), (4, 48), (8, 48)):
            width, rest = divmod(tiles, blocks * (depth // 16))
            if rest == 0 and 128 * width <= ruler.shape[2]:
                view = ruler.at[0:blocks, 0:depth, 0 : 128 * width]
                return self.net.copy(view, view, self.net.someone, self.at)
        raise ValueError(tiles)

    def wait_recv(self):
        self.whole().wait_recv()

    def wait_send(self):
        self.whole().wait_send()


def place_of(zb, z):
    return (zb - z + PLACES[0] + 8) % 8


def greet(devices):
    barrier = pltpu.get_barrier_semaphore()
    for device in devices:
        pl.semaphore_signal(barrier, inc=1, device_id=device, device_id_type=MESH)
    return lambda: pl.semaphore_wait(barrier, len(devices))


def lanes(start, size):
    return pl.ds(pl.multiple_of(start, 128), size)


def rows16(start, size):
    return pl.ds(pl.multiple_of(start, 16), size)


def arrive(copies):
    for copy in copies:
        copy.wait_recv()


def dot(a, b, dims=NN):
    return lax.dot_general(a, b, dims, preferred_element_type=F32)


def by_rows(step, carry=0):
    def one(i, carry):
        return step(pl.ds(pl.multiple_of(i * CHUNK, CHUNK), CHUNK), carry)

    return lax.fori_loop(0, ROWS // CHUNK, one, carry)


def stats(values):
    center = values - jnp.mean(values, -1, keepdims=True)
    return center, lax.rsqrt(jnp.mean(center * center, -1, keepdims=True) + eps)


def fold(values):
    return jnp.sum(values.reshape(-1, 8, values.shape[-1]), 0)


def norm_into(out, source, gain, bias):
    def step(r, carry):
        center, scale = stats(source[r, :].astype(F32))
        out[r, :] = (center * scale * gain + bias).astype(BF)
        return carry

    by_rows(step)


def norm_back(source, slope, gain, grad, low):
    def step(r, carry):
        center, scale = stats(source[r, :].astype(F32))
        unit = center * scale
        up = slope[r, :]
        inner = up * gain
        inner_mean = jnp.mean(inner, -1, keepdims=True)
        along = jnp.mean(inner * unit, -1, keepdims=True)
        new = grad[r, :] + scale * (inner - inner_mean - unit * along)
        grad[r, :] = new
        low[r, :] = new.astype(BF)
        return carry[0] + fold(up * unit), carry[1] + fold(up)

    zero = jnp.zeros((8, D), F32)
    sums = by_rows(step, (zero, zero))
    return tuple(jnp.sum(s, 0, keepdims=True) for s in sums)


def head_mean(values, spread):
    high = values.astype(BF)
    low = (values - high.astype(F32)).astype(BF)
    return dot(jnp.concatenate([high, low], 1), spread)


def split_heads(values, first):
    zero = jnp.zeros_like(values)
    return jnp.concatenate([jnp.where(first, values, zero), jnp.where(first, zero, values)], 0)


def join_heads(values, first):
    half = values.shape[0] // 2
    return jnp.where(first, values[:half], values[half:])


def first_half(rows):
    return lax.broadcasted_iota(jnp.int32, (rows, 128), 1) < HD


def spread_matrix():
    a = lax.broadcasted_iota(jnp.int32, (256, 128), 0) // HD % 2
    b = lax.broadcasted_iota(jnp.int32, (256, 128), 1) // HD
    return jnp.where(a == b, 1.0 / HD, 0.0).astype(BF)


def make_masks(lengths, mask):
    at_row = lax.broadcasted_iota(jnp.int32, (128, 128), 0)
    at_col = lax.broadcasted_iota(jnp.int32, (128, 128), 1)
    for r in range(2):
        end = jnp.int32(0)
        left = jnp.zeros((128, 128), jnp.int32)
        right = jnp.zeros((128, 128), jnp.int32)
        for p in range(4):
            end = end + lengths[r, p]
            left = left + jnp.where(at_row >= end, 1, 0)
            right = right + jnp.where(at_col >= end, 1, 0)
        same = jnp.where(left == right, 1.0, 0.0)
        mask[r, 0:128, :] = same
        mask[r, 128:256, :] = same


def gelu_and_slope(before):
    inner_scale, cubic = 0.7978845608028654, 0.044715
    square = before * before
    tanh = jnp.tanh(inner_scale * before * (1.0 + cubic * square))
    half = 0.5 * (1.0 + tanh)
    slope = half + 0.5 * before * (1.0 - tanh * tanh) * inner_scale * (1.0 + 3.0 * cubic * square)
    return before * half, slope


def gain_rows(gains, layer):
    return tuple(gains[layer, i : i + 1, :] for i in range(6))


class Gather:
    def __init__(self, me, net, w1, wd, nz):
        self.me, self.net, self.w1, self.wd, self.nz = me, net, w1, wd, nz
        self.sibling, self.xs, self.ys, self.zs = me.neighbours()
        self.chunks = [self.chunk(layer, kind) for layer in range(LAYERS) for kind in KINDS]
        every = [(i, k) for i in range(len(self.chunks)) for k in range(7)]
        self.turns = sorted(every, key=lambda turn: (STARTS_AT[turn[0]] + turn[1], turn[0]))
        self.done = 0

    def chunk(self, layer, kind):
        me, w1, wd = self.me, self.w1, self.wd
        down = kind == "down"
        base = 96 * me.c if down else STARTS[kind] + HALF * me.c

        def q(at, k):
            if down:
                return wd.at[layer, :, at, rows16(base + 16 * k, 16), :]
            return w1.at[layer, :, at, :, lanes(base + QUARTER * k, QUARTER)]

        def p(at, k):
            if down:
                return wd.at[layer, k[0], at, rows16(base + 64 + 16 * k[1], 16), :]
            return w1.at[layer, k[0], at, :, lanes(base + C_START + C_WIDTH * k[1], C_WIDTH)]

        def a(at):
            return w1.at[layer, :, at, :, lanes(base + A_START, A_WIDTH)]

        def whole(at):
            if down:
                return wd.at[layer, :, at, rows16(base, 96), :]
            return w1.at[layer, :, at, :, lanes(base, HALF)]

        long = 1 if kind == "up" else -1
        pieces = [(lambda at: q(at, me.y), long), (lambda at: p(at, me.on_x(0)), -long)]
        return SimpleNamespace(
            pieces=pieces, fours=((q, me.on_y, self.ys), (p, me.on_x, self.xs)), whole=whole,
            spare=[] if down else [(a, 1)], norms=layer == 0 and kind == "qkvo", first={}, second=[],
            moving=None, aside=None, norm_moving=[], shared=None,
        )

    def ring(self, pieces, k):
        batch = self.net.batch()
        for view, long in pieces:
            for d in (1, -1):
                if k < 4 or d == long:
                    batch.put(view(PLACES[-d * (k - 1)]), view(PLACES[-d * k]), self.zs[d])
        return batch

    def norm_ring(self, k):
        copies = []
        for d in (1, -1):
            if k < 4 or d == 1:
                block = self.nz.at[(self.me.z - d * (k - 1) + 8) % 8]
                copies.append(self.net.put(block, block, self.zs[d]))
        return copies

    def spread(self, chunk, group):
        batch = self.net.batch()
        for at in GROUPS[group]:
            for view, place, devices in chunk.fours if at is not None else ():
                for d in (1, -1):
                    batch.put(view(at, place(0)), view(at, place(0)), devices[d])
        chunk.first[group] = batch

    def relay(self, chunk, group):
        chunk.first[group].wait_recv()
        batch = self.net.batch()
        for d, at in zip((1, -1), GROUPS[group]):
            for view, place, devices in chunk.fours if at is not None else ():
                block = view(at, place(-d))
                batch.put(block, block, devices[d])
        chunk.second.append(batch)

    def tick(self, chunk, k):
        if 1 <= k <= 4:
            chunk.moving.wait_recv()
            arrive(chunk.norm_moving)
        if k < 4:
            chunk.moving = self.ring(chunk.pieces, k + 1)
            chunk.norm_moving = self.norm_ring(k + 1) if chunk.norms else []
        if k < 5:
            self.spread(chunk, k)
        if 1 <= k <= 5:
            self.relay(chunk, k - 1)
        if chunk.spare and k >= 2:
            if k > 2:
                chunk.aside.wait_recv()
            if k <= 5:
                chunk.aside = self.ring(chunk.spare, k - 1)
        if k == 2:
            chunk.shared = self.net.batch()
            chunk.shared.grows = True
        if k >= 2:
            chunk.second[k - 2].wait_recv()
            for at in GROUPS[k - 2]:
                if at is not None:
                    chunk.shared.put(chunk.whole(at), chunk.whole(at), self.sibling)
            if k == 6:
                chunk.shared.grows = False

    def nudge(self):
        for i, k in self.turns[self.done : self.done + 1]:
            if self.done < EARLY:
                self.net.settle(max(0, len(self.net.sent) - 16))
            self.tick(self.chunks[i], k)
            self.done += 1

    def complete(self, i):
        while (i, 6) not in self.turns[: self.done]:
            self.nudge()
        self.nudge()
        self.chunks[i].shared.wait_recv()


STARTS_AT = (0, 0.5, 2, 3, 4, 4.5)
EARLY = 24
GATHER_COPIES = 130
SAVED = ("normed", "unit", "scales", "values", "probs", "mixed", "middle", "second", "hidden", "slope")


def forward_kernel(
    qkv_ref, out_ref, up_ref, wd_ref, norm_ref, tokens, lengths,
    act, w1_out, wd_out, gains, stream_out, *rest,
):
    saved_out, rest = dict(zip(SAVED, rest)), rest[len(SAVED) :]
    kept, rest = dict(zip(SAVED, rest)), rest[len(SAVED) :]
    w1, wd, xf, stream, mask, raw, line, nc, nx, nz, send, recv, local, out_sem, save_sem = rest
    normed, unit, scales, values, probs, mixed, middle, second, hidden, slope = (kept[name] for name in SAVED)
    me = Place()
    x, y, z, c, xl, xh = me.x, me.y, me.z, me.c, me.xl, me.xh
    sibling, xs, ys, zs = me.neighbours()
    met = greet([sibling, xs[1], xs[-1], ys[1], ys[-1], zs[1], zs[-1]])
    net = Net(send, recv, sibling, w1.at[0, 0])

    for i, kind in enumerate(STARTS):
        mine = xf.at[i, :, pl.ds(24 * c, 24), :]
        if kind == "up":
            pltpu.make_async_copy(up_ref.at[:, :, lanes(c * HALF, HALF)], mine, local.at[i]).start()
    nc[c] = jnp.zeros((56, 128), F32)
    line[...] = jnp.zeros((8, 256), F32)
    line[0:2, 0:100] = norm_ref[...].astype(BF).astype(F32)
    first = 100 * lax.axis_index("shard")
    for layer in range(LAYERS):
        row = pltpu.roll(jnp.broadcast_to(line[layer : layer + 1, :], (8, 256)), first % 128, 1)
        for i in range(2):
            nc[c, pl.ds(25 * layer + first // 128 + i, 1), :] = row[0:1, 128 * i : 128 * i + 128]
    own_q, own_h = rows16(16 * y, 16), rows16(64 + 16 * xh, 16)
    own_qd = wd.at[:, xl, PLACES[0], rows16(96 * c + 16 * y, 16), :]
    own_qd[...] = wd_ref[:, own_q, :].astype(BF)
    wd[:, xl, PLACES[0], rows16(96 * c + 64 + 16 * xh, 16), :] = wd_ref[:, own_h, :].astype(BF)
    make_masks(lengths, mask)
    met()
    norm_swap = net.put(nc.at[c], nc.at[c], sibling)
    arrivals = []
    for i, kind in enumerate(STARTS):
        mine = xf.at[i, :, pl.ds(24 * c, 24), :]
        if kind == "up":
            net.put(up_ref.at[:, :, lanes((1 - c) * HALF, HALF)], mine, sibling)
        else:
            at = net.reserve()

            def parts(core):
                if core == 0:
                    return [(qkv_ref.at[:, :, 0:HALF], mine)]
                return [
                    (qkv_ref.at[:, :, HALF : 3 * D], mine.at[:, :, 0:D]),
                    (out_ref, mine.at[:, :, D:HALF]),
                ]

            for core in range(2):

                @pl.when(c == core)
                def _():
                    for src, dst in parts(core):
                        pltpu.make_async_copy(src, dst, local.at[i]).start()
                    for src, dst in parts(1 - core):
                        net.copy(src, dst, sibling, at).start()

            net.sent.append(net.copy(mine, mine, sibling, at))
        arrivals.append((pltpu.make_async_copy(mine, mine, local.at[i]), net.sent[-1]))
    cross = [net.put(own_qd, own_qd, xs[-1])]
    norm_swap.wait_recv()
    nx[xl] = nc[0] + nc[1]
    cross.append(net.put(nx.at[xl], nx.at[xl], xs[1]))
    for i, start in enumerate(STARTS.values()):
        base = start + c * HALF
        arrivals[i][0].wait()
        arrivals[i][1].wait_recv()
        own_q1 = w1.at[:, xl, PLACES[0], :, lanes(base + QUARTER * y, QUARTER)]
        own_a1 = w1.at[:, xl, PLACES[0], :, lanes(base + A_START, A_WIDTH)]
        own_q1[...] = xf[i, :, :, lanes(QUARTER * y, QUARTER)].astype(BF)
        own_a1[...] = xf[i, :, :, A_START : A_START + A_WIDTH].astype(BF)
        cross.append(net.put(own_q1, own_q1, xs[1]))
        cross.append(net.put(own_a1, own_a1, xs[-1]))
        w1[:, xl, PLACES[0], :, lanes(base + C_START + C_WIDTH * xh, C_WIDTH)] = xf[
            i, :, :, lanes(C_START + C_WIDTH * xh, C_WIDTH)
        ].astype(BF)
    arrive(cross)
    nz[z] = nx[0] + nx[1]
    moves = Gather(me, net, w1, wd, nz)
    outs = []

    def out(src, dst, sem):
        outs.append(pltpu.make_async_copy(src, dst, sem))
        outs[-1].start()

    def save(layer, *names):
        for name in names:
            out(kept[name].at[layer], saved_out[name].at[layer], save_sem.at[layer, SAVED.index(name)])

    def wide(layer, start, size):
        cols = lanes(start, size)
        return jnp.concatenate([w1[layer, r, place_of(zb, z), :, cols] for r in range(2) for zb in range(RING)], 0)

    def place_gains():
        total = nz[0]
        for i in range(1, 8):
            total = total + nz[i]
        for layer in range(LAYERS):
            for kind in range(4):
                for k in range(6):
                    at = 25 * layer + 6 * kind + k
                    gains[layer, kind : kind + 1, 128 * k : 128 * k + 128] = total[at : at + 1, :]
            pair = total[25 * layer + 24 : 25 * layer + 25, :]
            turned = pltpu.roll(pair, HD, 1)
            first = first_half(1)
            for kind, both in ((4, jnp.where(first, pair, turned)), (5, jnp.where(first, turned, pair))):
                for k in range(6):
                    gains[layer, kind : kind + 1, 128 * k : 128 * k + 128] = both
            gains[layer, 6:8, :] = jnp.zeros((2, D), F32)

    def forward(layer):
        source = tokens if layer == 0 else stream
        moves.complete(3 * layer)
        out(w1.at[layer, :, :, :, 0 : 4 * D], w1_out.at[layer, :, :, :, 0 : 4 * D], out_sem.at[layer, 0])
        if layer == 0:
            place_gains()
        gain_one, bias_one, gain_two, bias_two, gain_query, gain_key = gain_rows(gains, layer)
        norm_into(normed.at[layer], source, gain_one, bias_one)
        for part in range(3):
            joined = dot(normed[layer], wide(layer, D * part, D))
            if part < 2:
                raw[part] = joined
            else:
                values[layer] = joined.astype(BF)
            moves.nudge()
        save(layer, "normed", "values")
        pair_gains = (gain_query[:, 0:128], gain_key[:, 0:128])
        spread = spread_matrix()
        first_one = first_half(128)

        def attend(p):
            at = pl.ds(p * 128, 128)
            low_parts = []
            for part in range(2):
                whole = raw[part, :, at]
                center = whole - head_mean(whole, spread)
                scale = lax.rsqrt(head_mean(center * center, spread) + eps)
                normal = center * scale
                unit[layer, part, :, at] = normal
                scales[layer, part, :, at] = scale.astype(BF)
                low_parts.append((normal * pair_gains[part]).astype(BF))
            queries, keys = low_parts
            for r in range(2):
                rows = slice(128 * r, 128 * r + 128)
                both = split_heads(queries[rows], first_one)
                scores = dot(both, keys[rows], NT) * HD ** (-0.5)
                scores = jnp.where(mask[r] > 0.5, scores, -1e30)
                exponent = jnp.exp(scores - jnp.max(scores, -1, keepdims=True))
                probability = exponent * (1.0 / jnp.sum(exponent, -1, keepdims=True))
                probs[layer, r, p] = probability
                result = dot(probability.astype(BF), values[layer, rows, at])
                mixed[layer, rows, at] = join_heads(result, first_one).astype(BF)

        for p in range(PAIRS):
            attend(p)
            if p % 3 == 2:
                moves.nudge()
                moves.nudge()
        save(layer, "unit", "scales", "probs", "mixed")
        middle[layer] = source[...].astype(F32) + dot(mixed[layer], wide(layer, 3 * D, D))
        norm_into(second.at[layer], middle.at[layer], gain_two, bias_two)
        save(layer, "middle", "second")
        moves.nudge()

        def fourth(t):
            cols = lanes(FOURTH * t, FOURTH)
            raw[0] = dot(second[layer], wide(layer, 4 * D + FOURTH * t, FOURTH))

            def activate(r, carry):
                value, derivative = gelu_and_slope(raw[0, r, :])
                hidden[layer, r, cols] = value.astype(BF)
                slope[layer, r, cols] = derivative.astype(BF)
                return carry

            by_rows(activate)

        moves.complete(3 * layer + 1)
        out(w1.at[layer, :, :, :, 4 * D : 8 * D], w1_out.at[layer, :, :, :, 4 * D : 8 * D], out_sem.at[layer, 3])
        for t in range(4):
            fourth(t)
            moves.nudge()
        save(layer, "hidden", "slope")
        moves.complete(3 * layer + 2)
        for zb in range(RING):
            pltpu.make_async_copy(
                wd.at[layer, :, place_of(zb, z)], wd_out.at[layer, :, zb], out_sem.at[layer, 1]
            ).start()
        outs.append(pltpu.make_async_copy(wd.at[layer], wd_out.at[layer], out_sem.at[layer, 1]))
        whole = jnp.concatenate([wd[layer, r, place_of(zb, z)] for r in range(2) for zb in range(RING)], 0)
        result = middle[layer] + dot(hidden[layer], whole)
        if layer + 1 < LAYERS:
            stream[...] = result
            out(stream, stream_out, out_sem.at[layer, 2])
        else:
            act[...] = result.astype(BF)

    for layer in range(LAYERS):
        forward(layer)
    for copy in outs:
        copy.wait()
    net.finish()


def saved_shapes():
    pair = (2, ROWS, D)
    shapes = {
        "normed": ((ROWS, D), BF), "unit": (pair, F32), "scales": (pair, BF), "values": ((ROWS, D), BF),
        "probs": ((2, PAIRS, 256, 128), F32), "mixed": ((ROWS, D), BF), "middle": ((ROWS, D), F32),
        "second": ((ROWS, D), BF), "hidden": ((ROWS, FF), BF), "slope": ((ROWS, FF), BF),
    }
    return [shapes[name] for name in SAVED]


def forward_pass(qkv, out, up, down, norms, tokens, lengths):
    any_spec, vmem_spec = pl.BlockSpec(memory_space=pl.ANY), pl.BlockSpec(memory_space=pltpu.VMEM)
    smem_spec = pl.BlockSpec(memory_space=pltpu.SMEM)
    saved = [((LAYERS, *shape), kind) for shape, kind in saved_shapes()]
    outs = pl.pallas_call(
        forward_kernel,
        out_shape=(
            jax.ShapeDtypeStruct((ROWS, D), BF),
            jax.ShapeDtypeStruct((LAYERS, 2, RING, BLOCK, WIDE), BF),
            jax.ShapeDtypeStruct((LAYERS, 2, RING, DBLOCK, D), BF),
            jax.ShapeDtypeStruct((LAYERS, 8, D), F32),
            jax.ShapeDtypeStruct((ROWS, D), F32),
            *[jax.ShapeDtypeStruct(*item) for item in saved],
        ),
        in_specs=[any_spec, any_spec, any_spec, vmem_spec, vmem_spec, vmem_spec, smem_spec],
        out_specs=(vmem_spec, any_spec, any_spec, vmem_spec, any_spec, *[any_spec] * len(saved)),
        scratch_shapes=[
            *[pltpu.VMEM(*item) for item in saved],
            pltpu.VMEM((LAYERS, 2, RING, BLOCK, WIDE), BF),
            pltpu.VMEM((LAYERS, 2, RING, DBLOCK, D), BF),
            pltpu.VMEM((2, LAYERS, BLOCK, HALF), F32),
            pltpu.VMEM((ROWS, D), F32),
            pltpu.VMEM((2, 256, 128), F32),
            pltpu.VMEM((2, ROWS, D), F32),
            pltpu.VMEM((8, 256), F32),
            pltpu.VMEM((2, 56, 128), F32),
            pltpu.VMEM((2, 56, 128), F32),
            pltpu.VMEM((8, 56, 128), F32),
            pltpu.SemaphoreType.DMA((GATHER_COPIES,)),
            pltpu.SemaphoreType.DMA((GATHER_COPIES,)),
            pltpu.SemaphoreType.DMA((2,)),
            pltpu.SemaphoreType.DMA((LAYERS, 4)),
            pltpu.SemaphoreType.DMA((LAYERS, len(SAVED))),
        ],
        compiler_params=pltpu.CompilerParams(
            collective_id=0, has_side_effects=True, vmem_limit_bytes=63 * 1024 * 1024
        ),
        name="gather_and_forward",
    )(qkv, out, up, down, norms, tokens, lengths)
    return outs[0], outs[1], outs[2], outs[3], outs[4], outs[5:]


HALVES = (slice(4, 8), slice(0, 4))
PARTS = tuple((slice(7 - i, 8 - i), slice(i, i + 1)) for i in range(4))
SCATTER_COPIES = 150
SUM_ORDER = tuple((layer, kind) for layer in (1, 0) for kind in ("down", "up", "qkvo"))


class Scatter:
    def __init__(self, me, net, grads, buffers, sems):
        self.me, self.net, self.grads, self.b = me, net, grads, buffers
        self.local, self.swap_send, self.swap_recv, self.credit = sems
        self.sibling, self.xs, self.ys, self.zs = me.neighbours()
        self.chunks = [self.chunk(i, layer, kind) for i, (layer, kind) in enumerate(SUM_ORDER)]
        self.kept, self.swapped, self.turns = [], [], 0

    def chunk(self, index, layer, kind):
        me, b, down = self.me, self.b, kind == "down"
        own = b["own_" + kind]

        def q(at, k):
            if down:
                return own.at[layer, :, at, rows16(16 * k, 16), :]
            return own.at[layer, :, at, :, lanes(QUARTER * k, QUARTER)]

        def p(at, k):
            if down:
                return own.at[layer, k[0], at, rows16(64 + 16 * k[1], 16), :]
            return own.at[layer, k[0], at, :, lanes(C_START + C_WIDTH * k[1], C_WIDTH)]

        def a(at):
            return own.at[layer, :, at, :, A_START : A_START + A_WIDTH]

        def q_buffer(name):
            return lambda at: b[name + kind].at[layer, :, at]

        def p_buffer(name):
            return lambda at: b[name + kind].at[layer, at]

        def z_pair(name):
            return {1: (b["zp" + name + kind], layer), -1: (b["zm" + name + kind], layer)}

        fours = [
            (q, me.on_y, self.ys, *[q_buffer(name) for name in ("yf_", "yp_", "ym_")]),
            (p, me.on_x, self.xs, *[p_buffer(name) for name in ("xf_", "xp_", "xm_")]),
        ]
        long = 1 if kind == "up" else -1
        chain = [
            (lambda at: q(at, me.y), long, z_pair("q_")),
            (lambda at: p(at, me.on_x(0)), -long, z_pair("p_")),
        ]
        spare = [] if down else [(a, 1, z_pair("a_"))]
        return SimpleNamespace(
            index=index, layer=layer, kind=kind, fours=fours, chain=chain, spare=spare,
            far={}, second={}, near=None, moving=None, aside=None, at=0, ready=False,
        )

    def mine_and_theirs(self, chunk):
        return self.b["own_" + chunk.kind].at[chunk.layer], self.b["sib_" + chunk.kind]

    def swap_copy(self, chunk, src, dst):
        i = chunk.index
        return pltpu.make_async_remote_copy(
            src, dst, self.swap_send.at[i], self.swap_recv.at[i], device_id=self.sibling, device_id_type=MESH
        )

    def load(self, chunk):
        layer, c, kind = chunk.layer, self.me.c, chunk.kind
        mine, theirs = self.mine_and_theirs(chunk)
        sem = self.local.at[chunk.index]
        if kind != "qkvo":
            grad = self.grads[kind][layer]

            def half(core):
                if kind == "down":
                    return grad.at[:, :, rows16(96 * core, 96), :]
                return grad.at[:, :, :, lanes(HALF * core, HALF)]

            pltpu.make_async_copy(half(c), mine, sem).start()
            self.swap_copy(chunk, half(1 - c), theirs).start()
            return
        qkv, out = (self.grads[name][layer] for name in ("qkv", "out"))

        def parts(core, to):
            if core == 0:
                return [(qkv.at[:, :, :, 0:HALF], to)]
            return [(qkv.at[:, :, :, HALF : 3 * D], to.at[:, :, :, 0:D]), (out, to.at[:, :, :, D:HALF])]

        for core in range(2):

            @pl.when(c == core)
            def _():
                for src, dst in parts(core, mine):
                    pltpu.make_async_copy(src, dst, sem).start()
                for src, dst in parts(1 - core, theirs):
                    self.swap_copy(chunk, src, dst).start()

    def loaded(self, chunk):
        mine, theirs = self.mine_and_theirs(chunk)
        pltpu.make_async_copy(mine, mine, self.local.at[chunk.index]).wait()
        self.swap_copy(chunk, mine, theirs).wait_recv()

        def add(i, carry):
            for rows in range(2):
                mine[rows, i] = mine[rows, i] + theirs[rows, i]
            return carry

        lax.fori_loop(0, RING, add, 0)

    @staticmethod
    def sum_into(ref, *others):
        total = ref[...]
        for other in others:
            total = total + other[...]
        ref[...] = total

    def four_far(self, chunk, part):
        chunk.far[part] = self.net.batch()
        for d, at in zip((1, -1), PARTS[part]):
            for view, k, devices, first, ahead, behind in chunk.fours:
                chunk.far[part].put(view(at, k(2)), first(at), devices[d])

    def four_near(self, chunk):
        chunk.near = self.net.batch()
        for d, at in zip((1, -1), HALVES):
            for view, k, devices, first, ahead, behind in chunk.fours:
                back = ahead if d == -1 else behind
                chunk.near.put(view(at, k(-d)), back(at), devices[-d])

    def four_second(self, chunk, part):
        chunk.far[part].wait_recv()
        chunk.second[part] = self.net.batch()
        for d, at in zip((1, -1), PARTS[part]):
            for view, k, devices, first, ahead, behind in chunk.fours:
                block, front = view(at, k(d)), ahead if d == 1 else behind
                self.sum_into(block, first(at))
                chunk.second[part].put(block, front(at), devices[d])

    def four_last(self, chunk, part):
        if part == 0:
            chunk.near.wait_recv()
        chunk.second[part].wait_recv()
        for at in PARTS[part]:
            for view, k, devices, first, ahead, behind in chunk.fours:
                self.sum_into(view(at, k(0)), ahead(at), behind(at))

    def chain_step(self, pieces, k, before):
        if before:
            before.wait_recv()
        batch = self.net.batch()
        for view, long, buffers in pieces:
            for d in (1, -1):
                if k == 1 and d != long:
                    continue
                block = view(PLACES[d * (5 - k)])
                buffer, layer = buffers[d]
                if k > 2 or k == 2 and d == long:
                    self.sum_into(block, buffer.at[k - 2, layer])
                batch.put(block, buffer.at[k - 1, layer], self.zs[d])
        return batch

    def chain_last(self, pieces, before):
        before.wait_recv()
        for view, long, buffers in pieces:
            self.sum_into(view(PLACES[0]), *[buffers[d][0].at[3, buffers[d][1]] for d in (1, -1)])

    def begin(self, i):
        chunk = self.chunks[i]
        if chunk.layer == 0:
            while self.chunks[i - 3].at < 1:
                self.tick(self.chunks[i - 3])
            pl.semaphore_wait(self.credit.at[KINDS.index(chunk.kind)], 1)
        self.load(chunk)
        chunk.ready, chunk.begun = True, self.turns

    def tick(self, chunk):
        t = chunk.at
        chunk.at += 1
        if t > 6:
            self.to_copies(chunk) if t == 7 else self.to_sibling(chunk)
            return
        if t == 0:
            self.loaded(chunk)
            if chunk.layer == 1:
                pl.semaphore_signal(
                    self.credit.at[KINDS.index(chunk.kind)], inc=1, device_id=self.sibling, device_id_type=MESH
                )
        if t < 4:
            self.four_far(chunk, t)
        if t == 0:
            self.four_near(chunk)
        if 1 <= t <= 4:
            self.four_second(chunk, t - 1)
        if 2 <= t <= 5:
            self.four_last(chunk, t - 2)
        if 2 <= t < 6:
            chunk.moving = self.chain_step(chunk.chain, t - 1, chunk.moving)
        if t < 4 and chunk.spare:
            chunk.aside = self.chain_step(chunk.spare, t + 1, chunk.aside)
        if t == 6:
            if chunk.spare:
                self.chain_last(chunk.spare, chunk.aside)
            self.chain_last(chunk.chain, chunk.moving)
            self.over_copies(chunk)

    def slots(self, chunk, name):
        return self.b[name + chunk.kind].at[chunk.layer]

    @staticmethod
    def sum_slots(slots):
        total = slots[0].astype(F32)
        for i in range(1, 4):
            total = total + slots[i].astype(F32)
        return total.astype(BF)

    def over_copies(self, chunk):
        me, net, layer, down = self.me, self.net, chunk.layer, chunk.kind == "down"
        x, y, z, xl, xh = me.x, me.y, PLACES[0], me.xl, me.xh
        own = self.b["own_" + chunk.kind]

        def part_q(k):
            if down:
                return own.at[layer, k, z, rows16(16 * y, 16), :]
            return own.at[layer, k, z, :, lanes(QUARTER * y, QUARTER)]

        def part_a(k):
            return own.at[layer, k, z, :, A_START : A_START + A_WIDTH]

        over_x, over_y = net.batch(), net.batch()
        for view, name in ((part_q, "xs_"), (part_a, "xa_"))[: 1 if down else 2]:
            slots = self.slots(chunk, name)
            for d in (1, -1, 2):
                over_x.put(view(xl if d == 2 else 1 - xl), slots.at[x], self.xs[d])
            slots[x] = view(xl)[...]
        if down:
            part_p = own.at[layer, xl, z, rows16(64 + 16 * xh, 16), :]
        else:
            part_p = own.at[layer, xl, z, :, lanes(C_START + C_WIDTH * xh, C_WIDTH)]
        slots = self.slots(chunk, "ys_")
        for d in (1, -1, 2):
            over_y.put(part_p, slots.at[y], self.ys[d])
        slots[y] = part_p[...]
        chunk.over = (over_x, over_y)

    def to_copies(self, chunk):
        me, net, down = self.me, self.net, chunk.kind == "down"
        x, y, xh = me.x, me.y, me.xh
        total = self.b["out_down" if down else "rb_" + chunk.kind].at[chunk.layer]
        over_x, over_y = chunk.over
        last = net.batch()
        over_x.wait_recv()
        if not down:
            slots = self.slots(chunk, "ya_")
            slots[y] = self.sum_slots(self.slots(chunk, "xa_"))
            for d in (1, -1, 2):
                last.put(slots.at[y], slots.at[y], self.ys[d])
        mine = total.at[rows16(16 * y, 16), :] if down else total.at[:, lanes(QUARTER * y, QUARTER)]
        mine[...] = self.sum_slots(self.slots(chunk, "xs_"))
        for d in (1, -1, 2):
            last.put(mine, mine, self.ys[d])
        over_y.wait_recv()
        if down:
            mine = total.at[rows16(64 + 16 * xh, 16), :]
        else:
            mine = total.at[:, lanes(C_START + C_WIDTH * xh, C_WIDTH)]
        mine[...] = self.sum_slots(self.slots(chunk, "ys_"))
        last.put(mine, mine, self.xs[2])
        chunk.last = last

    def to_sibling(self, chunk):
        chunk.last.wait_recv()
        kind, layer, c = chunk.kind, chunk.layer, self.me.c
        if kind == "down":
            return
        total, wide = self.b["rb_" + kind].at[layer], self.b["rf_" + kind].at[layer]
        total[:, A_START : A_START + A_WIDTH] = self.sum_slots(self.slots(chunk, "ya_"))
        wide[...] = total[...].astype(F32)
        target = self.b["out_wide"].at[layer, :, lanes(STARTS[kind] + c * HALF, HALF)]
        self.swapped.append(self.net.put(wide.at[pl.ds(24 * (1 - c), 24), :], target, self.sibling))
        keep = pltpu.make_async_copy(wide.at[pl.ds(24 * c, 24), :], target, self.local.at[6 + len(self.kept)])
        keep.start()
        self.kept.append(keep)

    def turn(self, rest=None):
        self.turns += 1
        rest = GAP if rest is None else rest
        open_chunks = [ch for ch in self.chunks if ch.ready and ch.at < 9]
        rested = [ch for ch in open_chunks if self.turns - ch.begun >= (rest if ch.at else rest and REST)]
        for chunk in sorted(rested, key=lambda ch: SUM_AFTER[ch.index] + ch.at)[:AT_ONCE]:
            chunk.begun = self.turns
            self.tick(chunk)
        return bool(open_chunks)

    def swaps_sent(self):
        for chunk in self.chunks:
            self.swap_copy(chunk, *self.mine_and_theirs(chunk)).wait_send()


SUM_AFTER = (0, 2, 4, 6, 8, 10)
REST = 4
GAP = 3
AT_ONCE = 5
SETTLE, SETTLE_FIRST = 20, 8


def buffer_shapes():
    shapes = {}
    for kind in KINDS:
        rows, cols = (96, D) if kind == "down" else (BLOCK, HALF)
        quarter = (16, D) if kind == "down" else (BLOCK, QUARTER)
        half = (16, D) if kind == "down" else (BLOCK, C_WIDTH)
        shapes["own_" + kind] = (2, 2, RING, rows, cols)
        shapes["sib_" + kind] = (2, RING, rows, cols)
        for name in ("yf_", "yp_", "ym_"):
            shapes[name + kind] = (2, 2, RING, *quarter)
        for name in ("xf_", "xp_", "xm_"):
            shapes[name + kind] = (2, RING, *half)
        for name in ("zp", "zm"):
            shapes[name + "q_" + kind] = (4, 2, 2, *quarter)
            shapes[name + "p_" + kind] = (4, 2, *half)
        shapes["xs_" + kind] = (2, 4, *quarter)
        shapes["ys_" + kind] = (2, 4, *half)
        if kind != "down":
            for name in ("zp", "zm"):
                shapes[name + "a_" + kind] = (4, 2, 2, BLOCK, A_WIDTH)
            shapes["xa_" + kind] = shapes["ya_" + kind] = (2, 4, BLOCK, A_WIDTH)
            shapes["rb_" + kind] = (2, BLOCK, HALF)
    return shapes


BUFFERS = buffer_shapes()
WEIGHT_SLOTS = 3
STAGE_SLOTS = 2
GRAD_SHAPES = {"qkv": (D, 3 * D), "out": (D, D), "up": (D, FF), "down": (FF, D)}


def backward_kernel(tokens, cotangent, gains, w1_ref, wd_ref, stream_ref, *rest):
    saved, rest = dict(zip(SAVED, rest)), rest[len(SAVED) :]
    input_grad, out1, outd, outn = rest[:4]
    grads_flat, rest = rest[4:12], rest[12:]
    names = tuple(GRAD_SHAPES)
    grads = {name: grads_flat[2 * i : 2 * i + 2] for i, name in enumerate(names)}
    kept, rest = dict(zip(SAVED, rest)), rest[len(SAVED) :]
    b, rest = dict(zip(BUFFERS, rest)), rest[len(BUFFERS) :]
    (
        rf, stream, weight, low, wide_low, grad, slow, turned, stage, gn, norm_sum, nc, nz, ny, nx,
        send, recv, local, swap_send, swap_recv, credit, load_sem, weight_sem, store_sem, plain_sem,
    ) = rest
    unit, scales, values, probs = (kept[name] for name in ("unit", "scales", "values", "probs"))
    me = Place()
    x, y, z, c, xl, xh = me.x, me.y, me.z, me.c, me.xl, me.xh
    sibling, xs, ys, zs = me.neighbours()

    met = greet([sibling, *xs.values(), *ys.values(), *zs.values()])
    use_order = ("hidden", "slope", "second", "middle", "mixed", "probs", "values", "unit", "scales", "normed")
    fetched = {}

    def fetch(layer, *wanted):
        for name in wanted:
            fetched[name] = pltpu.make_async_copy(
                saved[name].at[layer], kept[name], load_sem.at[SAVED.index(name)]
            )
            fetched[name].start()

    wide_weight = weight.reshape(WEIGHT_SLOTS, 2, RING, BLOCK, D)
    tall_weight = weight.reshape(WEIGHT_SLOTS, 4, DBLOCK, D)
    weight_views = []
    for layer in reversed(range(LAYERS)):
        for t in range(4):
            weight_views.append((wd_ref.at[layer, t // 2, t % 2 * 4 : t % 2 * 4 + 4], tall_weight))
        for start in (*[4 * D + FOURTH * t for t in range(4)], 3 * D, 0, D, 2 * D):
            weight_views.append((w1_ref.at[layer, :, :, :, start : start + D], wide_weight))
    weight_copies = []

    def ask_weight():
        n = len(weight_copies)
        if n < len(weight_views):
            slot = n % WEIGHT_SLOTS
            view, to = weight_views[n]
            weight_copies.append(pltpu.make_async_copy(view, to.at[slot], weight_sem.at[slot]))
            weight_copies[-1].start()

    taken = []

    def take_weight():
        n = len(taken)
        taken.append(n)
        weight_copies[n].wait()
        slot = n % WEIGHT_SLOTS
        if weight_views[n][1] is tall_weight:
            return weight[slot]
        return jnp.concatenate(
            [wide_weight[slot, r, place_of(zb, z)] for r in range(2) for zb in range(RING)], 0
        )

    first_copies = [
        pltpu.make_async_copy(cotangent, low, plain_sem.at[0]),
        pltpu.make_async_copy(stream_ref, stream, plain_sem.at[1]),
    ]
    first_copies[0].start()
    ask_weight()
    fetch(1, *use_order[:2])
    for i in range(WEIGHT_SLOTS - 1):
        ask_weight()
    fetch(1, *use_order[2:])
    first_copies[1].start()

    net = Net(send, recv, sibling, b["own_qkvo"].at[0, 0])
    shaped = {name: grads[name] for name in names}
    b.update(out_down=outd, out_wide=out1, rf_qkvo=rf.at[0], rf_up=rf.at[1])
    sums = Scatter(me, net, shaped, b, (local, swap_send, swap_recv, credit))

    pending = {}
    count = [0]

    def flush():
        for copy in pending.values():
            copy.wait()
        pending.clear()

    def emit(value, name, layer, start, by_row):
        slot = count[0] % STAGE_SLOTS
        count[0] += 1
        if slot in pending:
            pending.pop(slot).wait()
        target, low_value = grads[name][layer], value.astype(BF)
        whole = stage.at[slot]
        if by_row:
            stage[slot] = low_value
            for i in range(4):
                row = start // DBLOCK + i
                pltpu.make_async_copy(
                    stage.at[slot, DBLOCK * i : DBLOCK * i + DBLOCK],
                    target.at[row // RING, place_of(row % RING, z)],
                    store_sem.at[slot],
                ).start()
            pending[slot] = pltpu.make_async_copy(whole, whole, store_sem.at[slot])
            return
        src = stage.at[slot].reshape(2, RING, BLOCK, D)
        for row in range(2 * RING):
            src[row // RING, place_of(row % RING, z)] = low_value[BLOCK * row : BLOCK * row + BLOCK]
        pending[slot] = pltpu.make_async_copy(src, target.at[:, :, :, start : start + D], store_sem.at[slot])
        pending[slot].start()

    def put_rows(layer, kind, rows):
        for i, row in enumerate(rows):
            for k in range(6):
                at = 25 * layer + 6 * (kind + i) + k
                gn[at : at + 1, :] = row[:, 128 * k : 128 * k + 128]

    def backward(layer):
        again = layer > 0
        gain_one, bias_one, gain_two, bias_two, gain_query, gain_key = gain_rows(gains, layer)
        slope, hidden = kept["slope"], kept["hidden"]
        fetched["hidden"].wait()
        fetched["slope"].wait()
        for t in range(4):
            cols = slice(FOURTH * t, FOURTH * t + FOURTH)
            grad_hidden = dot(low[...], take_weight(), NT)
            wide_low[:, cols] = (slope[:, cols].astype(F32) * grad_hidden).astype(BF)
            ask_weight()
            turned[...] = hidden[:, cols].T
            emit(dot(turned[...], low[...]), "down", layer, FOURTH * t, True)
            sums.turn()
        fetched["second"].wait()
        turned[...] = kept["second"][...].T
        if again:
            fetch(layer - 1, "slope", "hidden", "second")
        for t in range(4):
            cols = slice(FOURTH * t, FOURTH * t + FOURTH)
            part = dot(wide_low[:, cols], take_weight(), NT)
            slow[...] = part if t == 0 else slow[...] + part
            ask_weight()
            if t == 0:
                flush()
                if layer == 1:
                    met()
                sums.begin(0 if layer == 1 else 3)
            emit(dot(turned[...], wide_low[:, cols]), "up", layer, FOURTH * t, False)
            sums.turn()
        flush()
        sums.begin(1 if layer == 1 else 4)
        fetched["middle"].wait()
        put_rows(layer, 2, norm_back(kept["middle"], slow, gain_two, grad, low))
        fetched["mixed"].wait()
        turned[...] = kept["mixed"][...].T
        if again:
            fetch(layer - 1, "middle", "mixed")
        emit(dot(turned[...], low[...]), "out", layer, 0, False)
        wide_low[:, 3 * D : 4 * D] = dot(low[...], take_weight(), NT).astype(BF)
        ask_weight()
        sums.turn()
        for name in ("probs", "values", "unit", "scales"):
            fetched[name].wait()
        pair_gains = (gain_query[:, 0:128], gain_key[:, 0:128])
        spread = spread_matrix()
        first_one = first_half(128)

        def attend(p, carry):
            at = pl.ds(p * 128, 128)
            normals = [unit[part, :, at] for part in range(2)]
            queries, keys = ((normals[part] * pair_gains[part]).astype(BF) for part in range(2))
            slopes = ([], [])
            for r in range(2):
                rows = slice(128 * r, 128 * r + 128)
                both = split_heads(queries[rows], first_one)
                grad_both = split_heads(wide_low[rows, pl.ds(3 * D + p * 128, 128)], first_one)
                probability = probs[r, p]
                grad_values = dot(probability.astype(BF), grad_both, TN)
                wide_low[rows, pl.ds(2 * D + p * 128, 128)] = grad_values.astype(BF)
                grad_probs = dot(grad_both, values[rows, at], NT)
                weighted = grad_probs * probability
                inner = jnp.sum(weighted, -1, keepdims=True)
                grad_scores = (weighted - probability * inner).astype(BF)
                slopes[0].append(join_heads(dot(grad_scores, keys[rows]), first_one) * HD ** (-0.5))
                slopes[1].append(dot(grad_scores, both, TN) * HD ** (-0.5))
            sums_now = []
            for part in range(2):
                up = jnp.concatenate(slopes[part], 0)
                normal = normals[part]
                sums_now.append(carry[part] + fold(up * normal))
                inner = up * pair_gains[part]
                along = head_mean(inner * normal, spread)
                result = scales[part, :, at].astype(F32) * (inner - head_mean(inner, spread) - normal * along)
                wide_low[:, pl.ds(part * D + p * 128, 128)] = result.astype(BF)
            return tuple(sums_now)

        zero = jnp.zeros((8, 128), F32)
        head_sums = (zero, zero)
        for p in range(PAIRS):
            head_sums = attend(p, head_sums)
            if p % 3 == 2:
                sums.turn()
        totals = []
        for part in head_sums:
            total = jnp.sum(part, 0, keepdims=True)
            totals.append(total + pltpu.roll(total, HD, 1))
        gn[25 * layer + 24 : 25 * layer + 25, :] = jnp.where(first_half(1), *totals)
        if again:
            fetch(layer - 1, "probs", "values", "unit", "scales")
        fetched["normed"].wait()
        turned[...] = kept["normed"][...].T
        if again:
            fetch(layer - 1, "normed")
        for part in range(3):
            cols = slice(D * part, D * part + D)
            emit(dot(turned[...], wide_low[:, cols]), "qkv", layer, D * part, False)
            sums.turn()
        flush()
        sums.begin(2 if layer == 1 else 5)
        for part in range(3):
            cols = slice(D * part, D * part + D)
            piece = dot(wide_low[:, cols], take_weight(), NT)
            slow[...] = piece if part == 0 else slow[...] + piece
            ask_weight()
        if layer == 1:
            first_copies[1].wait()
        put_rows(layer, 0, norm_back(stream if layer == 1 else tokens, slow, gain_one, grad, low))

    first_copies[0].wait()

    def turn(r, carry):
        grad[r, :] = low[r, :].astype(F32)
        return carry

    by_rows(turn)
    gn[...] = jnp.zeros(gn.shape, F32)
    for layer in reversed(range(LAYERS)):
        backward(layer)
    grad_out = pltpu.make_async_copy(low, input_grad, plain_sem.at[0])
    grad_out.start()

    nc[c] = gn[...]
    norm_swap = net.put(gn, nc.at[c], sibling)
    norm_moving = [norm_swap]

    def norm_ring(k):
        copies = []
        for d in (1, -1):
            if k < 4 or d == 1:
                slot = nz.at[(z - d * (k - 1) + 8) % 8]
                copies.append(net.put(slot, slot, zs[d]))
        return copies

    t = 0
    while sums.turn(0) or t < 7:
        net.settle(SETTLE if sums.chunks[-2].at > 8 else SETTLE_FIRST)
        arrive(norm_moving)
        norm_moving = []
        if t == 0:
            nz[z] = nc[0] + nc[1]
        if t < 4:
            norm_moving = norm_ring(t + 1)
        elif t == 4:
            total = nz[0]
            for i in range(1, 8):
                total = total + nz[i]
            ny[y] = total
            norm_moving = [net.put(ny.at[y], ny.at[y], ys[d]) for d in (1, -1, 2)]
        elif t == 5:
            nx[x] = ny[0] + ny[1] + ny[2] + ny[3]
            norm_moving = [net.put(nx.at[x], nx.at[x], xs[d]) for d in (1, -1, 2)]
        elif t == 6:
            norm_sum[0:56, :] = nx[0] + nx[1] + nx[2] + nx[3]
        t += 1

    arrive(sums.swapped)
    shard = lax.axis_index("shard")
    for row, (layer, first) in enumerate(((0, 100 * shard), (1, 100 * shard), (0, 3 * D + 24 * shard), (1, 3 * D + 24 * shard))):
        at = 25 * layer + first // 128
        pair = [jnp.broadcast_to(norm_sum[pl.ds(at + i, 1), :], (8, 128)) for i in range(2)]
        turned_row = pltpu.roll(jnp.concatenate(pair, 1), (256 - first % 128) % 256, 1)
        outn[row : row + 1, :] = turned_row[0:1, 0:128]
    outn[4:8, :] = jnp.zeros((4, 128), F32)
    for copy in sums.kept:
        copy.wait()
    grad_out.wait()
    net.finish()
    sums.swaps_sent()


def backward_pass(tokens, cotangent, gains, w1, wd, stream, saved):
    any_spec, vmem_spec = pl.BlockSpec(memory_space=pl.ANY), pl.BlockSpec(memory_space=pltpu.VMEM)
    grad_shapes = [
        (2, RING, shape[0] // 16, shape[1]) for shape in GRAD_SHAPES.values() for layer in range(LAYERS)
    ]
    outs = pl.pallas_call(
        backward_kernel,
        out_shape=(
            jax.ShapeDtypeStruct((ROWS, D), BF),
            jax.ShapeDtypeStruct((LAYERS, 24, WIDE), F32),
            jax.ShapeDtypeStruct((LAYERS, 96, D), BF),
            jax.ShapeDtypeStruct((8, 128), F32),
            *[jax.ShapeDtypeStruct(shape, BF) for shape in grad_shapes],
        ),
        in_specs=[vmem_spec, any_spec, vmem_spec, any_spec, any_spec, any_spec, *[any_spec] * len(SAVED)],
        out_specs=(any_spec, any_spec, vmem_spec, vmem_spec, *[any_spec] * len(grad_shapes)),
        scratch_shapes=[
            *[pltpu.VMEM(*item) for item in saved_shapes()],
            *[pltpu.VMEM(shape, BF) for shape in BUFFERS.values()],
            pltpu.VMEM((2, 2, BLOCK, HALF), F32),
            pltpu.VMEM((ROWS, D), F32),
            pltpu.VMEM((WEIGHT_SLOTS, D, D), BF),
            pltpu.VMEM((ROWS, D), BF),
            pltpu.VMEM((ROWS, FF), BF),
            pltpu.VMEM((ROWS, D), F32),
            pltpu.VMEM((ROWS, D), F32),
            pltpu.VMEM((D, ROWS), BF),
            pltpu.VMEM((STAGE_SLOTS, D, D), BF),
            pltpu.VMEM((56, 128), F32),
            pltpu.VMEM((64, 128), F32),
            pltpu.VMEM((2, 56, 128), F32),
            pltpu.VMEM((8, 56, 128), F32),
            pltpu.VMEM((4, 56, 128), F32),
            pltpu.VMEM((4, 56, 128), F32),
            pltpu.SemaphoreType.DMA((SCATTER_COPIES,)),
            pltpu.SemaphoreType.DMA((SCATTER_COPIES,)),
            pltpu.SemaphoreType.DMA((10,)),
            pltpu.SemaphoreType.DMA((6,)),
            pltpu.SemaphoreType.DMA((6,)),
            pltpu.SemaphoreType.REGULAR((3,)),
            pltpu.SemaphoreType.DMA((len(SAVED),)),
            pltpu.SemaphoreType.DMA((WEIGHT_SLOTS,)),
            pltpu.SemaphoreType.DMA((STAGE_SLOTS,)),
            pltpu.SemaphoreType.DMA((2,)),
        ],
        compiler_params=pltpu.CompilerParams(
            collective_id=1, has_side_effects=True, vmem_limit_bytes=63 * 1024 * 1024
        ),
        name="backward_and_scatter",
    )(tokens, cotangent, gains, w1, wd, stream, *saved)
    return outs[:4]


STEPS = 3
FACTOR = 65536 ** (-0.5)


def updated(gradient_sum, master, moment, average):
    gradient_scaled = gradient_sum * FACTOR
    moment_new = momentum_decay * moment + gradient_scaled
    master_new = master - learn_rate * (gradient_scaled + momentum_decay * moment_new)
    average_new = average_decay * average + (1.0 - average_decay) * master_new
    return master_new, moment_new, average_new, master_new.astype(BF)


def update_kernel(*refs):
    ins, outs = refs[:22], refs[22:]
    for i in range(5):
        sums, old, new = ins[4 * i], ins[4 * i + 1 : 4 * i + 4], outs[4 * i : 4 * i + 4]
        total = sums[0:2, 0:100] if i == 4 else sums[...].astype(F32)
        for ref, value in zip(new, updated(total, *[ref[...] for ref in old])):
            ref[...] = value
    for i in range(2):
        outs[20 + i][...] = ins[20 + i][...]
    outs[22][...] = ins[16][2:4, 0:24] * FACTOR


def update(sums, states, rows):
    in_specs, out_specs, shapes, args = [], [], [], []
    starts = (0, 3 * D, 4 * D, 0, 0)
    for start, total, state in zip(starts, sums, states):
        shape = state[0].shape
        if len(shape) == 2:
            block, place = shape, lambda i: (0, 0)
            total_block, total_place = total.shape, place
        elif shape[1] == 96:
            block, place = (shape[0], shape[1] // STEPS, shape[2]), lambda i: (0, i, 0)
            total_block, total_place = block, place
        else:
            block, place = (*shape[:2], shape[2] // STEPS), lambda i: (0, 0, i)
            total_block, total_place = block, lambda i, first=start // (shape[2] // STEPS): (0, 0, first + i)
        spec = pl.BlockSpec(block, place)
        in_specs += [pl.BlockSpec(total_block, total_place), spec, spec, spec]
        out_specs += [spec] * 4
        shapes += [jax.ShapeDtypeStruct(shape, kind) for kind in (F32, F32, F32, BF)]
        args += [total, *state]
    row_spec = pl.BlockSpec((ROWS, D // STEPS), lambda i: (0, i))
    shift = (LAYERS, 24)
    return pl.pallas_call(
        update_kernel,
        grid=(STEPS,),
        out_shape=[*shapes, *[jax.ShapeDtypeStruct((ROWS, D), BF)] * 2, jax.ShapeDtypeStruct(shift, F32)],
        in_specs=[*in_specs, row_spec, row_spec],
        out_specs=[*out_specs, row_spec, row_spec, pl.BlockSpec(shift, lambda i: (0, 0))],
        compiler_params=pltpu.CompilerParams(vmem_limit_bytes=63 * 1024 * 1024),
        name="update",
    )(*args, *rows)


def body(
    tokens, cotangent, picture_lengths, w_qkv, mom_qkv, ema_qkv, w_out, mom_out, ema_out, w_up, mom_up, ema_up,
    w_down, mom_down, ema_down, norms, mom_norms, ema_norms,
):
    flat_tokens = tokens.reshape(ROWS, D)
    act, w1, wd, gains, stream, saved = forward_pass(
        w_qkv, w_out, w_up, w_down, norms, flat_tokens, picture_lengths.reshape(2, 4)
    )
    input_grad, sum1, sumd, sumn = backward_pass(
        flat_tokens, cotangent.reshape(ROWS, D), gains, w1, wd, stream, saved
    )
    outs = update(
        (sum1, sum1, sum1, sumd, sumn),
        (
            (w_qkv, mom_qkv, ema_qkv), (w_out, mom_out, ema_out), (w_up, mom_up, ema_up),
            (w_down, mom_down, ema_down), (norms, mom_norms, ema_norms),
        ),
        (act, input_grad),
    )
    return (outs[20].reshape(tokens.shape), outs[21].reshape(tokens.shape), *outs[:20], outs[22])


def solution(mesh):
    rows = P(None, ("shard", "rep"), None, None)
    wide, flat = P(None, "shard", None), P(None, "shard")
    return jax.shard_map(
        body,
        mesh=mesh,
        in_specs=(rows, rows, P(None, ("shard", "rep"), None), *[wide] * 12, *[flat] * 3),
        out_specs=(rows, rows, *[wide] * 16, *[flat] * 5),
        check_vma=False,
    )
```
